128 devices in a mesh: seq: 16 (over y, x), ep: 8 (over z, core).
Axes of the slice: x: 4, y: 4, z: 4, core: 2. Of those that a mesh axis runs over, the one named last changes fastest.
Arguments:
- tokens: bfloat16 [16384, 2560], P(('seq', 'ep')), may hold values from -6 to 6
- expert_ids: int32 [16384, 6], P(('seq', 'ep')), may hold values from 0 to 23, as said below
- devices: int32 [16384, 3], P(('seq', 'ep')), may hold values from 0 to 7, as said below
- slots: int32 [16384, 3], P(('seq', 'ep')), may hold values from -1 to 11, as said below
- gates: float32 [16384, 6], P(('seq', 'ep')), may hold values from 0.05 to 0.5
- w_gate: bfloat16 [24, 2560, 2048], P('ep', None, 'seq'), may hold values from -0.125 to 0.125
- w_up: bfloat16 [24, 2560, 2048], P('ep', None, 'seq'), may hold values from -0.125 to 0.125
- w_down: bfloat16 [24, 2048, 2560], P('ep', 'seq'), may hold values from -0.125 to 0.125
- shared_gate: bfloat16 [2560, 2048], P(None, 'ep'), may hold values from -0.125 to 0.125
- shared_up: bfloat16 [2560, 2048], P(None, 'ep'), may hold values from -0.125 to 0.125
- shared_down: bfloat16 [2560, 2048], P(None, 'ep'), may hold values from -0.125 to 0.125
Outputs:
- moe_out: bfloat16 [16384, 2560], P(('seq', 'ep'))
The draws below stay inside these ranges and needn't reach their ends.
Inputs may be any that keep to these rules, and one draw needn't show every extreme that they name: Each token names 3 different devices of ep. `expert_ids`: the 6 ids of a token differ, and id // 3 is one of the token's devices; a device of the token may hold none of them. `slots`: among the tokens of one device, taken in token order, the first 12 of those that name device d of ep get 0, 1, 2 and so on up to 11 in the matching entry; any later ones get -1 and are dropped.
All inputs are finite; a program needn't handle non-finite values.
Results may differ from the reference program's by a relative error of at most 0.018.
Values may be sent and summed in bfloat16 or wider, within the bound.
A program may use at most 192 MiB of HBM per device.

```python
import math
import jax
import jax.numpy as jnp
from jax import lax

D = 2560
FF_DEV = 128
SH_DEV = 256
EXP_DEV = 3
TOP = 6
MAX_DEV = 3
TOK_DEV = 128
CAP = 12
FF = 2048
SH = 2048
EXPERTS = 24
TOKENS = 16384
N_SEQ = 16
N_EP = 8


def routing(key):
    key_popular, key_scores, key_experts = jax.random.split(key, 3)
    popular = jax.random.randint(key_popular, (N_EP,), 0, 3) * 256
    scores = jax.random.randint(key_scores, (TOKENS, N_EP), 0, 1024) + popular[None, :]
    scores = scores * N_EP + jnp.arange(N_EP, dtype=jnp.int32)[None, :]
    _, chosen = lax.top_k(scores, MAX_DEV)
    chosen = chosen.astype(jnp.int32)
    choices = MAX_DEV * EXP_DEV
    expert_scores = jax.random.randint(key_experts, (TOKENS, choices), 0, 1 << 20) * choices + jnp.arange(choices, dtype=jnp.int32)[None, :]
    _, picked = lax.top_k(expert_scores, TOP)
    picked = picked.astype(jnp.int32)
    owners = jnp.take_along_axis(chosen, picked // EXP_DEV, axis=1)
    expert_ids = (owners * EXP_DEV + picked % EXP_DEV).astype(jnp.int32)
    naming = jnp.any(chosen[:, :, None] == jnp.arange(N_EP, dtype=jnp.int32)[None, None, :], axis=1).astype(jnp.int32)
    blocked = naming.reshape(TOKENS // TOK_DEV, TOK_DEV, N_EP)
    before = (jnp.cumsum(blocked, axis=1) - blocked).reshape(TOKENS, N_EP)
    ranks = jnp.take_along_axis(before, chosen, axis=1)
    slot_index = jnp.where(ranks < CAP, ranks, -1).astype(jnp.int32)
    return (chosen, expert_ids, slot_index)


def draw_devices(key, part):
    return routing(key)[0]


def draw_expert_ids(key, part):
    return routing(key)[1]


def draw_slots(key, part):
    return routing(key)[2]


def levels(rng, extent, pieces, smallest, largest):
    def one(dim, shards_of):
        steps = jax.random.uniform(jax.random.fold_in(jax.random.fold_in(rng, 6), dim), (shards_of,), jnp.float32, smallest / len(pieces), largest / len(pieces))
        return jnp.repeat(jnp.exp(steps), extent[dim] // shards_of).reshape((-1,) + (1,) * (len(extent) - dim - 1))

    loudness = one(*pieces[0])
    for cut in pieces[1:]:
        loudness = loudness * one(*cut)
    return loudness


def centred(key, shape, scale, bound, shards=(), kind=jnp.bfloat16):
    gain = levels(key, shape, shards, -0.22, 0.18) if shards else 1.0
    result = jax.random.normal(key, shape, jnp.float32) * scale * gain
    return jnp.minimum(jnp.maximum(result, -bound), bound).astype(kind)


def setup_inputs(seed: int = 0) -> dict:
    key_list = jax.random.split(jax.random.key(seed), 12)
    tokens = centred(key_list[0], (TOKENS, D), 1.0, 6.0, ((0, 128),))
    expert_ids = draw_expert_ids(jax.random.fold_in(key_list[11], 71), 0)
    devices = draw_devices(jax.random.fold_in(key_list[11], 71), 0)
    slots = draw_slots(jax.random.fold_in(key_list[11], 71), 0)
    gates = jnp.clip(jnp.exp(math.log(0.5) - 2.3025851 * jax.random.uniform(key_list[4], (TOKENS, TOP), jnp.float32) ** levels(key_list[4], (TOKENS, TOP), ((0, 128),), -0.2, 0.2)), 0.05, 0.5)
    w_gate = centred(key_list[5], (EXPERTS, D, FF), D ** -0.5, 0.125, ((0, 8), (2, 16)))
    w_up = centred(key_list[6], (EXPERTS, D, FF), D ** -0.5, 0.125, ((0, 8), (2, 16)))
    w_down = centred(key_list[7], (EXPERTS, FF, D), FF ** -0.5, 0.125, ((0, 8), (1, 16)))
    shared_gate = centred(key_list[8], (D, SH), D ** -0.5, 0.125, ((1, 8),))
    shared_up = centred(key_list[9], (D, SH), D ** -0.5, 0.125, ((1, 8),))
    shared_down = centred(key_list[10], (D, SH), SH ** -0.5, 0.125, ((1, 8),))
    return {"tokens": tokens, "expert_ids": expert_ids, "devices": devices, "slots": slots, "gates": gates, "w_gate": w_gate, "w_up": w_up, "w_down": w_down, "shared_gate": shared_gate, "shared_up": shared_up, "shared_down": shared_down}


def local_gates(expert_ids, devices, gates):
    owners = devices[:, :, None] * EXP_DEV + jnp.arange(EXP_DEV, dtype=jnp.int32)[None, None, :]
    matches = expert_ids[:, None, None, :] == owners[:, :, :, None]
    summed = jnp.sum(jnp.where(matches, gates[:, None, None, :], jnp.float32(0.0)), axis=3)
    return summed.astype(jnp.bfloat16)


def swiglu(inputs, gate_block, up_block):
    first = jnp.dot(inputs, gate_block, preferred_element_type=jnp.float32)
    second = jnp.dot(inputs, up_block, preferred_element_type=jnp.float32)
    return jax.nn.silu(first) * second


def rounded(values):
    return lax.optimization_barrier(values.astype(jnp.bfloat16)).astype(jnp.float32)


def reference(tokens, expert_ids, devices, slots, gates, w_gate, w_up, w_down, shared_gate, shared_up, shared_down):
    total_rows = N_SEQ * N_EP * CAP
    slot_gate = local_gates(expert_ids, devices, gates)
    source = jnp.arange(TOKENS, dtype=jnp.int32) // TOK_DEV

    def column(running, device):
        landed = (devices == device) & (slots >= 0)
        row_index = jnp.where(landed, source[:, None] * CAP + slots, total_rows).astype(jnp.int32)
        slot_rows = jnp.zeros((total_rows, D), jnp.bfloat16)
        gate_rows = jnp.zeros((total_rows, EXP_DEV), jnp.bfloat16)
        for j in range(MAX_DEV):
            slot_rows = slot_rows.at[row_index[:, j]].set(tokens, mode="drop")
            gate_rows = gate_rows.at[row_index[:, j]].set(slot_gate[:, j], mode="drop")
        first = (device * EXP_DEV).astype(jnp.int32)
        gate_local = lax.dynamic_slice_in_dim(w_gate, first, EXP_DEV, 0)
        up_local = lax.dynamic_slice_in_dim(w_up, first, EXP_DEV, 0)
        down_local = lax.dynamic_slice_in_dim(w_down, first, EXP_DEV, 0)
        hidden = []
        for k in range(EXP_DEV):
            scaled = swiglu(slot_rows, gate_local[k], up_local[k]) * gate_rows[:, k:k + 1].astype(jnp.float32)
            hidden.append(scaled.astype(jnp.bfloat16))
        slot_sum = jnp.zeros((total_rows, D), jnp.float32)
        for b in range(N_SEQ):
            partial_value = jnp.zeros((total_rows, D), jnp.float32)
            for k in range(EXP_DEV):
                partial_value = partial_value + jnp.dot(hidden[k][:, b * FF_DEV:(b + 1) * FF_DEV], down_local[k, b * FF_DEV:(b + 1) * FF_DEV, :], preferred_element_type=jnp.float32)
            slot_sum = slot_sum + rounded(partial_value)
        slot_out = slot_sum.astype(jnp.bfloat16)
        for j in range(MAX_DEV):
            picked = jnp.take(slot_out, row_index[:, j], axis=0, mode="fill", fill_value=0)
            running = running + picked.astype(jnp.float32)
        return running, None

    routed, _ = lax.scan(column, jnp.zeros((TOKENS, D), jnp.float32), jnp.arange(N_EP, dtype=jnp.int32))
    shared = jnp.zeros((TOKENS, D), jnp.float32)
    for c in range(N_EP):
        block = slice(c * SH_DEV, (c + 1) * SH_DEV)
        shared_hidden = swiglu(tokens, shared_gate[:, block], shared_up[:, block]).astype(jnp.bfloat16)
        partial_value = lax.dot_general(shared_hidden, shared_down[:, block], (((1,), (1,)), ((), ())), preferred_element_type=jnp.float32)
        shared = shared + rounded(partial_value)
    return (shared + routed).astype(jnp.bfloat16)
```

```python
import functools

import jax
import jax.numpy as jnp
from jax import lax
from jax.experimental import pallas as pl
from jax.experimental.pallas import tpu as pltpu
from jax.sharding import PartitionSpec as P

MESH = pl.DeviceIdType.MESH
F32 = jnp.float32
BF16 = jnp.bfloat16

SIDE = 4
N_EP = 8
TOK = 128
D = 2560
WIDE = D + 128
CAP = 12
PIECE = 16
HALF = 4 * CAP
SH = 256
LEFT = 1280

HERE, NEXT, PREV, FAR = 0, 1, 2, 3


class Copies:
    def __init__(self, send, recv):
        self.send, self.recv, self.made = send, recv, []

    def start(self, src, dst, device):
        i = len(self.made)
        copy = pltpu.make_async_remote_copy(
            src_ref=src,
            dst_ref=dst,
            send_sem=self.send.at[i],
            recv_sem=self.recv.at[i],
            device_id=device,
            device_id_type=MESH,
        )
        copy.start()
        self.made.append(copy)
        return copy


def add_rows(dst, start, rows, cols, terms):
    @pl.loop(0, rows // 16)
    def _(i):
        at = pl.ds(pl.multiple_of(start + i * 16, 16), 16)
        total = dst[at, cols].astype(F32)
        for ref, first in terms:
            total += ref[pl.ds(pl.multiple_of(first + i * 16, 16), 16), cols].astype(F32)
        dst[at, cols] = total.astype(BF16)


def row(b, h, a):
    return ((b * 2 + h) * 4 + a) * HALF


def kernel(
    ids_ref,
    dev_ref,
    slot_ref,
    gates_ref,
    tok_hbm,
    wg_hbm,
    wu_hbm,
    wd_hbm,
    sg_hbm,
    su_hbm,
    sd_hbm,
    out_ref,
    wgu,
    wd,
    sgu,
    sd,
    send,
    land,
    xs,
    ys,
    hid,
    r1,
    r2,
    t1,
    t2,
    back,
    ret,
    shx,
    shp,
    shh,
    sib,
    u1,
    u2,
    send_sem,
    recv_sem,
    local_sem,
):
    seq, ep = lax.axis_index("seq"), lax.axis_index("ep")
    y, x = seq // SIDE, lax.rem(seq, SIDE)
    z, core = ep // 2, lax.rem(ep, 2)

    def up(v, by):
        return lax.rem(v + by, SIDE)

    xp, xm = (y * SIDE + up(x, 1), ep), (y * SIDE + up(x, 3), ep)
    yp, ym = (up(y, 1) * SIDE + x, ep), (up(y, 3) * SIDE + x, ep)
    zp, zm = (seq, up(z, 1) * 2 + core), (seq, up(z, 3) * 2 + core)
    twin = (seq, z * 2 + 1 - core)
    ep_to = [(seq, lax.rem(ep + r, N_EP)) for r in range(N_EP)]
    ep_from = [(seq, lax.rem(ep + N_EP - r, N_EP)) for r in range(N_EP)]
    rings = [((xp, xm), (yp, ym)), ((yp, ym), (xp, xm))]

    barrier = pltpu.get_barrier_semaphore()
    partners = [xp, xm, yp, ym] + ep_to[1:]
    for device in partners:
        pl.semaphore_signal(barrier, inc=1, device_id=device, device_id_type=MESH)

    loads = []

    def load(src, dst):
        copy = pltpu.make_async_copy(src, dst, local_sem.at[len(loads)])
        copy.start()
        loads.append(copy)
        return copy

    tok = shx.at[pl.ds(0, TOK)]
    load_tok = load(tok_hbm, tok)
    load_routed = []
    for k in range(3):
        load_routed.append(load(wg_hbm.at[k], wgu.at[k, :, pl.ds(0, 128)]))
        load_routed.append(load(wu_hbm.at[k], wgu.at[k, :, pl.ds(128, 128)]))
        load_routed.append(load(wd_hbm.at[k], wd.at[pl.ds(k * 128, 128)]))
    load_shared = [
        load(sg_hbm, sgu.at[:, pl.ds(0, SH)]),
        load(su_hbm, sgu.at[:, pl.ds(SH, SH)]),
        load(sd_hbm, sd),
    ]

    rows_i = lax.broadcasted_iota(jnp.int32, (TOK, TOK), 0)
    lanes_i = lax.broadcasted_iota(jnp.int32, (TOK, TOK), 1)
    place = jnp.zeros((TOK, TOK), F32)
    gate_of = [jnp.zeros((TOK, TOK), F32) for _ in range(3)]
    for j in range(3):
        dev = dev_ref[j : j + 1, :]
        slot = slot_ref[j : j + 1, :]
        turn = dev - ep
        turn = jnp.where(turn < 0, turn + N_EP, turn)
        target = jnp.where(slot >= 0, turn * PIECE + slot, -1)
        hit = rows_i == target
        place = jnp.where(hit, 1.0, place)
        for k in range(3):
            summed = jnp.zeros((1, TOK), F32)
            for r in range(6):
                summed += jnp.where(
                    ids_ref[r : r + 1, :] == dev * 3 + k, gates_ref[r : r + 1, :], 0.0
                )
            gate_of[k] = jnp.where(hit, summed, gate_of[k])
    place = place.astype(BF16)
    columns = jnp.zeros((TOK, TOK), F32)
    for k in range(3):
        column = jnp.sum(gate_of[k], axis=1, keepdims=True)
        columns = jnp.where(lanes_i == k, column, columns)
    send[:, D:] = columns.astype(BF16)

    load_tok.wait()
    for n in range(D // 512):
        cols = slice(n * 512, (n + 1) * 512)
        send[:, cols] = jnp.dot(place, shx[0:TOK, cols], preferred_element_type=F32).astype(BF16)

    pl.semaphore_wait(barrier, len(partners))
    copies = Copies(send_sem, recv_sem)

    arrive = [None] + [
        copies.start(
            send.at[pl.ds(r * PIECE, PIECE)], land.at[pl.ds(r * PIECE, PIECE)], ep_to[r]
        )
        for r in range(1, N_EP)
    ]
    land[0:PIECE, :] = send[0:PIECE, :]

    def dense(rows, cols, flip):
        one = lax.broadcasted_iota(jnp.int32, (rows, cols), 1 if flip else 0)
        two = lax.broadcasted_iota(jnp.int32, (rows, cols), 0 if flip else 1)
        hit = jnp.zeros((rows, cols), F32)
        for i in range(4):
            inside = (one >= CAP * i) & (one < CAP * (i + 1)) & (two == one + (PIECE - CAP) * i)
            hit = jnp.where(inside, 1.0, hit)
        return hit.astype(BF16)

    squeeze = dense(HALF, 4 * PIECE, False)
    spread = dense(4 * PIECE, HALF, True)

    def xb(b, h, a, n=1):
        return xs.at[pl.ds(row(b, h, a), n * HALF)]

    def yb(b, h, a, n=1):
        return ys.at[pl.ds(row(b, h, a), n * HALF)]

    gather = [[], []]
    for h in range(2):
        for r in range(4 * h, 4 * h + 4):
            if r:
                arrive[r].wait_recv()
        for n in range(WIDE // 384):
            cols = slice(n * 384, (n + 1) * 384)
            xs[row(HERE, h, HERE) : row(HERE, h, HERE) + HALF, cols] = jnp.dot(
                squeeze, land[h * 64 : h * 64 + 64, cols], preferred_element_type=F32
            ).astype(BF16)
        (ap, am), (bp, bm) = rings[h]
        own = xb(HERE, h, HERE)
        gather[h] += [
            copies.start(own, xb(HERE, h, PREV), ap),
            copies.start(own, xb(HERE, h, NEXT), am),
            copies.start(own, xb(PREV, h, HERE), bp),
            copies.start(own, xb(NEXT, h, HERE), bm),
        ]

    def sx(dz, c):
        return shx.at[pl.ds((c * 4 + dz) * TOK, TOK)]

    lo, hi = pl.ds(0, LEFT), pl.ds(LEFT, D - LEFT)
    wide_hi = pl.ds(LEFT, WIDE - LEFT)
    ring = [
        copies.start(sx(HERE, 0), sx(PREV, 0), zp),
        copies.start(sx(HERE, 0), sx(NEXT, 0), zm),
    ]
    to_twin = [copies.start(sx(HERE, 0), sx(HERE, 1), twin)]

    def part(ref, cols):
        return ref.at[:, cols]

    for h in range(2):
        (ap, am), (bp, bm) = rings[h]
        c = gather[h]
        c[0].wait_recv()
        c.append(copies.start(part(xb(HERE, h, PREV), lo), part(xb(HERE, h, FAR), lo), ap))
        c[1].wait_recv()
        c.append(
            copies.start(part(xb(HERE, h, NEXT), wide_hi), part(xb(HERE, h, FAR), wide_hi), am)
        )
        c.append(copies.start(xb(HERE, h, PREV), xb(PREV, h, PREV), bp))
        c.append(copies.start(xb(HERE, h, PREV), xb(NEXT, h, PREV), bm))
        c.append(copies.start(xb(HERE, h, NEXT), xb(PREV, h, NEXT), bp))
        c.append(copies.start(xb(HERE, h, NEXT), xb(NEXT, h, NEXT), bm))
    for h in range(2):
        (ap, am), (bp, bm) = rings[h]
        c = gather[h]
        c[2].wait_recv()
        c.append(None)
        c.append(None)
        c.append(copies.start(xb(PREV, h, HERE), xb(FAR, h, HERE), bp))
        c[4].wait_recv()
        c[5].wait_recv()
        c[10] = copies.start(xb(HERE, h, FAR), xb(PREV, h, FAR), bp)
        c[11] = copies.start(xb(HERE, h, FAR), xb(NEXT, h, FAR), bm)
    for h in range(2):
        (ap, am), (bp, bm) = rings[h]
        c = gather[h]
        c[8].wait_recv()
        c.append(copies.start(xb(PREV, h, NEXT), xb(FAR, h, NEXT), bp))
        c[7].wait_recv()
        c.append(copies.start(xb(NEXT, h, PREV), xb(FAR, h, PREV), bm))

    def forward_tokens():
        ring[0].wait_recv()
        ring.append(copies.start(part(sx(PREV, 0), lo), part(sx(FAR, 0), lo), zp))
        to_twin.append(copies.start(sx(PREV, 0), sx(PREV, 1), twin))
        ring[1].wait_recv()
        ring.append(copies.start(part(sx(NEXT, 0), hi), part(sx(FAR, 0), hi), zm))
        to_twin.append(copies.start(sx(NEXT, 0), sx(NEXT, 1), twin))

    def routed(b):
        at = pl.ds(row(b, 0, 0), 8 * HALF)
        gate = xs[at, D:].astype(F32)
        for k in range(3):
            both = jnp.dot(xs[at, 0:D], wgu[k], preferred_element_type=F32)
            value = jax.nn.silu(both[:, :128]) * both[:, 128:] * gate[:, k : k + 1]
            hid[:, k * 128 : (k + 1) * 128] = value.astype(BF16)

        @pl.loop(0, D // 512)
        def _(n):
            cols = pl.ds(pl.multiple_of(n * 512, 512), 512)
            ys[at, cols] = jnp.dot(hid[...], wd[:, cols], preferred_element_type=F32).astype(BF16)

    forward_tokens()
    for copy in load_routed:
        copy.wait()
    routed(HERE)
    for h in range(2):
        (ap, am), (bp, bm) = rings[h]
        c = gather[h]
        c[11].wait_recv()
        c.append(copies.start(xb(NEXT, h, FAR), xb(FAR, h, FAR), bm))
    for h in range(2):
        c = gather[h]
        for i in (6, 10, 3, 9):
            c[i].wait_recv()
    routed(PREV)
    reduce = [[None] * 10, [None] * 10]
    for h in range(2):
        (ap, am), (bp, bm) = rings[h]
        reduce[h][3] = copies.start(yb(PREV, h, HERE, 2), r2.at[h, 1, pl.ds(0, 2 * HALF)], bm)
    routed(NEXT)
    for h in range(2):
        (ap, am), (bp, bm) = rings[h]
        reduce[h][2] = copies.start(
            yb(NEXT, h, PREV, 2), r2.at[h, 0, pl.ds(2 * HALF, 2 * HALF)], bp
        )

    ring[2].wait_recv()
    ring[3].wait_recv()
    to_twin.append(copies.start(sx(FAR, 0), sx(FAR, 1), twin))
    for copy in load_shared:
        copy.wait()

    def shared(c):
        @pl.loop(0, 2)
        def _(i):
            at = pl.ds(pl.multiple_of(c * 4 * TOK + i * 2 * TOK, 2 * TOK), 2 * TOK)
            both = jnp.dot(shx[at, :], sgu[...], preferred_element_type=F32)
            shh[...] = (jax.nn.silu(both[:, :SH]) * both[:, SH:]).astype(BF16)

            @pl.loop(0, D // 512)
            def _(n):
                cols = pl.ds(pl.multiple_of(n * 512, 512), 512)
                shp[at, cols] = lax.dot_general(
                    shh[...], sd[cols, :], (((1,), (1,)), ((), ())), preferred_element_type=F32
                ).astype(BF16)

    for h in range(2):
        for i in range(12, 16):
            gather[h][i].wait_recv()
    routed(FAR)
    for h in range(2):
        (ap, am), (bp, bm) = rings[h]
        reduce[h][0] = copies.start(yb(FAR, h, HERE, 2), r1.at[h, 0], bp)
        reduce[h][1] = copies.start(yb(FAR, h, PREV, 2), r1.at[h, 1], bm)

    for copy in to_twin:
        copy.wait_recv()
    shared(1)
    sums = [
        copies.start(
            shp.at[pl.ds((4 + dz) * TOK, TOK)], sib.at[pl.ds(dz * TOK, TOK)], twin
        )
        for dz in range(4)
    ]
    every = pl.ds(0, D)
    for h in range(2):
        (ap, am), (bp, bm) = rings[h]
        c = reduce[h]
        c[0].wait_recv()
        add_rows(ys, row(NEXT, h, HERE), 2 * HALF, every, [(r1.at[h, 0], 0)])
        c[4] = copies.start(yb(NEXT, h, HERE, 2), r2.at[h, 0, pl.ds(0, 2 * HALF)], bp)
        c[1].wait_recv()
        add_rows(ys, row(PREV, h, PREV), 2 * HALF, every, [(r1.at[h, 1], 0)])
        c[5] = copies.start(yb(PREV, h, PREV, 2), r2.at[h, 1, pl.ds(2 * HALF, 2 * HALF)], bm)
    shared(0)
    for copy in sums:
        copy.wait_recv()
    add_rows(shp, 0, 4 * TOK, every, [(sib, 0)])

    def sp(dz):
        return shp.at[pl.ds(dz * TOK, TOK)]

    zs = [
        copies.start(part(sp(FAR), lo), part(u1, lo), zp),
        copies.start(part(sp(FAR), hi), part(u1, hi), zm),
    ]
    zs[0].wait_recv()
    add_rows(shp, NEXT * TOK, TOK, lo, [(u1, 0)])
    zs.append(copies.start(sp(NEXT), u2.at[0], zp))
    zs[1].wait_recv()
    add_rows(shp, PREV * TOK, TOK, hi, [(u1, 0)])
    zs.append(copies.start(sp(PREV), u2.at[1], zm))

    for h in range(2):
        (ap, am), (bp, bm) = rings[h]
        c = reduce[h]
        for i in (2, 3, 4, 5):
            c[i].wait_recv()
        add_rows(
            ys,
            row(HERE, h, HERE),
            4 * HALF,
            every,
            [(r2.at[h, 0], 0), (r2.at[h, 1], 0)],
        )
        c[6] = copies.start(part(yb(HERE, h, FAR), lo), part(t1.at[h], lo), ap)
        c[7] = copies.start(part(yb(HERE, h, FAR), hi), part(t1.at[h], hi), am)
    for h in range(2):
        (ap, am), (bp, bm) = rings[h]
        c = reduce[h]
        c[6].wait_recv()
        add_rows(ys, row(HERE, h, NEXT), HALF, lo, [(t1.at[h], 0)])
        c[8] = copies.start(yb(HERE, h, NEXT), t2.at[h, 0], ap)
        c[7].wait_recv()
        add_rows(ys, row(HERE, h, PREV), HALF, hi, [(t1.at[h], 0)])
        c[9] = copies.start(yb(HERE, h, PREV), t2.at[h, 1], am)

    home = []
    for h in range(2):
        c = reduce[h]
        c[8].wait_recv()
        c[9].wait_recv()
        first = row(HERE, h, HERE)
        add_rows(ys, first, HALF, every, [(t2.at[h, 0], 0), (t2.at[h, 1], 0)])
        for n in range(D // 512):
            cols = slice(n * 512, (n + 1) * 512)
            back[h * 64 : h * 64 + 64, cols] = jnp.dot(
                spread, ys[first : first + HALF, cols], preferred_element_type=F32
            ).astype(BF16)
        for r in range(4 * h, 4 * h + 4):
            piece = pl.ds(r * PIECE, PIECE)
            if r:
                home.append(copies.start(back.at[piece], ret.at[piece], ep_from[r]))
            else:
                ret[piece, :] = back[piece, :]

    for copy in zs[2:]:
        copy.wait_recv()
    for copy in home:
        copy.wait_recv()
    for n in range(D // 512):
        cols = slice(n * 512, (n + 1) * 512)
        total = lax.dot_general(
            place, ret[:, cols], (((0,), (0,)), ((), ())), preferred_element_type=F32
        )
        total += shp[0:TOK, cols].astype(F32)
        total += u2[0, :, cols].astype(F32) + u2[1, :, cols].astype(F32)
        out_ref[:, cols] = total.astype(BF16)

    for copy in copies.made:
        copy.wait_send()


def local(
    tokens,
    expert_ids,
    devices,
    slots,
    gates,
    w_gate,
    w_up,
    w_down,
    shared_gate,
    shared_up,
    shared_down,
):
    vmem = pl.BlockSpec(memory_space=pltpu.VMEM)
    anywhere = pl.BlockSpec(memory_space=pl.ANY)
    copies = 7 + 32 + 4 + 4 + 20 + 4 + 4 + 7
    return pl.pallas_call(
        kernel,
        out_shape=jax.ShapeDtypeStruct((TOK, D), BF16),
        in_specs=[vmem] * 4 + [anywhere] * 7,
        out_specs=vmem,
        scratch_shapes=[
            pltpu.VMEM((3, D, 256), BF16),
            pltpu.VMEM((384, D), BF16),
            pltpu.VMEM((D, 2 * SH), BF16),
            pltpu.VMEM((D, SH), BF16),
            pltpu.VMEM((TOK, WIDE), BF16),
            pltpu.VMEM((TOK, WIDE), BF16),
            pltpu.VMEM((32 * HALF, WIDE), BF16),
            pltpu.VMEM((32 * HALF, D), BF16),
            pltpu.VMEM((8 * HALF, 384), BF16),
            pltpu.VMEM((2, 2, 2 * HALF, D), BF16),
            pltpu.VMEM((2, 2, 4 * HALF, D), BF16),
            pltpu.VMEM((2, HALF, D), BF16),
            pltpu.VMEM((2, 2, HALF, D), BF16),
            pltpu.VMEM((TOK, D), BF16),
            pltpu.VMEM((TOK, D), BF16),
            pltpu.VMEM((8 * TOK, D), BF16),
            pltpu.VMEM((8 * TOK, D), BF16),
            pltpu.VMEM((2 * TOK, SH), BF16),
            pltpu.VMEM((4 * TOK, D), BF16),
            pltpu.VMEM((TOK, D), BF16),
            pltpu.VMEM((2, TOK, D), BF16),
            pltpu.SemaphoreType.DMA((copies,)),
            pltpu.SemaphoreType.DMA((copies,)),
            pltpu.SemaphoreType.DMA((16,)),
        ],
        compiler_params=pltpu.CompilerParams(
            collective_id=0, has_side_effects=True, vmem_limit_bytes=62 * 1024 * 1024
        ),
        cost_estimate=pl.CostEstimate(
            flops=13_100_000_000, bytes_accessed=12_000_000, transcendentals=900_000
        ),
    )(
        expert_ids.T,
        devices.T,
        slots.T,
        gates.T,
        tokens,
        w_gate,
        w_up,
        w_down,
        shared_gate,
        shared_up,
        shared_down,
    )


def solution(mesh):
    in_specs = (
        P(("seq", "ep"), None),
        P(("seq", "ep"), None),
        P(("seq", "ep"), None),
        P(("seq", "ep"), None),
        P(("seq", "ep"), None),
        P("ep", None, "seq"),
        P("ep", None, "seq"),
        P("ep", "seq", None),
        P(None, "ep"),
        P(None, "ep"),
        P(None, "ep"),
    )
    out_specs = P(("seq", "ep"), None)
    return jax.shard_map(local, mesh=mesh, in_specs=in_specs, out_specs=out_specs, check_vma=False)
```

```python
import functools

import jax
import jax.numpy as jnp
from jax import lax
from jax.experimental import pallas as pl
from jax.experimental.pallas import tpu as pltpu
from jax.sharding import PartitionSpec as P

MESH = pl.DeviceIdType.MESH
F32 = jnp.float32
BF16 = jnp.bfloat16

SIDE = 4
N_EP = 8
TOK = 128
D = 2560
WIDE = D + 128
CAP = 12
PIECE = 16
HALF = 4 * CAP
SH = 256
LEFT = 1280
MAIN = 1920
TAIL = D - MAIN
ORDER = (0, 1, 2, 7, 6, 3, 4, 5)

HERE, NEXT, PREV, FAR = 0, 1, 2, 3


class Copies:
    def __init__(self, send, recv):
        self.send, self.recv, self.made = send, recv, []

    def start(self, src, dst, device):
        i = len(self.made)
        copy = pltpu.make_async_remote_copy(
            src_ref=src,
            dst_ref=dst,
            send_sem=self.send.at[i],
            recv_sem=self.recv.at[i],
            device_id=device,
            device_id_type=MESH,
        )
        copy.start()
        self.made.append(copy)
        return copy


def add_rows(dst, start, rows, cols, terms):
    @pl.loop(0, rows // 16)
    def _(i):
        at = pl.ds(pl.multiple_of(start + i * 16, 16), 16)
        total = dst[at, cols].astype(F32)
        for ref, first in terms:
            total += ref[pl.ds(pl.multiple_of(first + i * 16, 16), 16), cols].astype(F32)
        dst[at, cols] = total.astype(BF16)


def row(b, h, a):
    return ((b * 2 + h) * 4 + a) * HALF


def kernel(
    ids_ref,
    dev_ref,
    slot_ref,
    gates_ref,
    tok_hbm,
    wg_hbm,
    wu_hbm,
    wd_hbm,
    sg_hbm,
    su_hbm,
    sd_hbm,
    out_ref,
    wgu,
    wd,
    sgu,
    sd,
    send,
    land,
    xs,
    ys,
    hid,
    r1,
    ahead,
    behind,
    t1,
    tahead,
    tbehind,
    back,
    ret,
    shx,
    shp,
    shh,
    sib,
    u1,
    u2,
    send_sem,
    recv_sem,
    local_sem,
):
    seq, ep = lax.axis_index("seq"), lax.axis_index("ep")
    y, x = seq // SIDE, lax.rem(seq, SIDE)
    z, core = ep // 2, lax.rem(ep, 2)

    def up(v, by):
        return lax.rem(v + by, SIDE)

    xp, xm = (y * SIDE + up(x, 1), ep), (y * SIDE + up(x, 3), ep)
    yp, ym = (up(y, 1) * SIDE + x, ep), (up(y, 3) * SIDE + x, ep)
    zp, zm = (seq, up(z, 1) * 2 + core), (seq, up(z, 3) * 2 + core)
    twin = (seq, z * 2 + 1 - core)
    ep_to = [(seq, lax.rem(ep + r, N_EP)) for r in range(N_EP)]
    ep_from = [(seq, lax.rem(ep + N_EP - r, N_EP)) for r in range(N_EP)]
    rings = [((xp, xm), (yp, ym)), ((yp, ym), (xp, xm))]

    barrier = pltpu.get_barrier_semaphore()
    partners = [xp, xm, yp, ym] + ep_to[1:]
    for device in partners:
        pl.semaphore_signal(barrier, inc=1, device_id=device, device_id_type=MESH)

    loads = []

    def load(src, dst):
        copy = pltpu.make_async_copy(src, dst, local_sem.at[len(loads)])
        copy.start()
        loads.append(copy)
        return copy

    tok = shx.at[pl.ds(0, TOK)]
    load_tok = load(tok_hbm, tok)
    load_routed = []
    for k in range(3):
        load_routed.append(load(wg_hbm.at[k], wgu.at[k, :, pl.ds(0, 128)]))
        load_routed.append(load(wu_hbm.at[k], wgu.at[k, :, pl.ds(128, 128)]))
        load_routed.append(load(wd_hbm.at[k], wd.at[pl.ds(k * 128, 128)]))
    load_shared = [
        load(sg_hbm, sgu.at[:, pl.ds(0, SH)]),
        load(su_hbm, sgu.at[:, pl.ds(SH, SH)]),
        load(sd_hbm, sd),
    ]

    rows_i = lax.broadcasted_iota(jnp.int32, (TOK, TOK), 0)
    lanes_i = lax.broadcasted_iota(jnp.int32, (TOK, TOK), 1)
    place = jnp.zeros((TOK, TOK), F32)
    place_tail = [jnp.zeros((TOK, TOK), F32) for _ in range(3)]
    gate_of = [jnp.zeros((TOK, TOK), F32) for _ in range(3)]
    for j in range(3):
        dev = dev_ref[j : j + 1, :]
        slot = slot_ref[j : j + 1, :]
        turn = dev - ep
        turn = jnp.where(turn < 0, turn + N_EP, turn)
        piece = jnp.where(turn < 3, turn, jnp.where(turn < 6, turn + 2, 10 - turn))
        hit = rows_i == jnp.where(slot >= 0, piece * PIECE + slot, -1)
        place = jnp.where(hit, 1.0, place)
        for g in range(3):
            mine = (slot >= 4 * g) & (slot < 4 * g + 4)
            tail_row = jnp.where(mine, piece * PIECE + CAP - 4 * g + slot, -1)
            place_tail[g] = jnp.where(rows_i == tail_row, 1.0, place_tail[g])
        for k in range(3):
            summed = jnp.zeros((1, TOK), F32)
            for r in range(6):
                summed += jnp.where(
                    ids_ref[r : r + 1, :] == dev * 3 + k, gates_ref[r : r + 1, :], 0.0
                )
            gate_of[k] = jnp.where(hit, summed, gate_of[k])
    place = place.astype(BF16)
    place_tail = [p.astype(BF16) for p in place_tail]
    columns = jnp.zeros((TOK, TOK), F32)
    for k in range(3):
        column = jnp.sum(gate_of[k], axis=1, keepdims=True)
        columns = jnp.where(lanes_i == k, column, columns)
    send[:, MAIN:] = columns.astype(BF16)

    load_tok.wait()
    for g in range(3):
        cols = slice(g * TAIL, (g + 1) * TAIL)
        send[:, cols] = (
            jnp.dot(place, shx[0:TOK, cols], preferred_element_type=F32)
            + jnp.dot(place_tail[g], shx[0:TOK, MAIN:], preferred_element_type=F32)
        ).astype(BF16)

    pl.semaphore_wait(barrier, len(partners))
    copies = Copies(send_sem, recv_sem)

    arrive = [None]
    for p in range(1, N_EP):
        piece = pl.ds(p * PIECE, PIECE)
        arrive.append(copies.start(send.at[piece], land.at[piece], ep_to[ORDER[p]]))
    land[0:PIECE, :] = send[0:PIECE, :]

    def dense(flip, g=None):
        shape = (4 * PIECE, HALF) if flip else (HALF, 4 * PIECE)
        one = lax.broadcasted_iota(jnp.int32, shape, 1 if flip else 0)
        two = lax.broadcasted_iota(jnp.int32, shape, 0 if flip else 1)
        hit = jnp.zeros(shape, F32)
        for i in range(4):
            first, count, shift = CAP * i, CAP, (PIECE - CAP) * i
            if g is not None:
                first, count, shift = first + 4 * g, 4, shift + CAP - 4 * g
            inside = (one >= first) & (one < first + count) & (two == one + shift)
            hit = jnp.where(inside, 1.0, hit)
        return hit.astype(BF16)

    squeeze, squeeze_tail = dense(False), [dense(False, g) for g in range(3)]
    spread, spread_tail = dense(True), [dense(True, g) for g in range(3)]

    lo, hi = pl.ds(0, LEFT), pl.ds(LEFT, D - LEFT)
    wide_hi = pl.ds(LEFT, WIDE - LEFT)

    def xb(b, h, a, cols):
        return xs.at[pl.ds(row(b, h, a), HALF), cols]

    streams = []
    for h in range(2):
        (ap, am), (bp, bm) = rings[h]
        streams.append((h, lo, lo, PREV, NEXT, ap, am, bp, bm))
        streams.append((h, wide_hi, hi, NEXT, PREV, am, ap, bm, bp))

    gather = [{} for _ in streams]
    for h in range(2):
        for p in range(4 * h, 4 * h + 4):
            if p:
                arrive[p].wait_recv()
        first = row(HERE, h, HERE)
        rows = slice(h * 64, h * 64 + 64)
        for g in range(3):
            cols = slice(g * TAIL, (g + 1) * TAIL)
            xs[first : first + HALF, cols] = jnp.dot(
                squeeze, land[rows, cols], preferred_element_type=F32
            ).astype(BF16)
        tail = jnp.zeros((HALF, TAIL), F32)
        for g in range(3):
            cols = slice(g * TAIL, (g + 1) * TAIL)
            tail += jnp.dot(squeeze_tail[g], land[rows, cols], preferred_element_type=F32)
        xs[first : first + HALF, MAIN:D] = tail.astype(BF16)
        xs[first : first + HALF, D:] = jnp.dot(
            squeeze, land[rows, MAIN:], preferred_element_type=F32
        ).astype(BF16)
        for i in (2 * h, 2 * h + 1):
            _, cols, _, near, next_, af, ab, bf, bb = streams[i]
            own, got = xb(HERE, h, HERE, cols), gather[i]
            got["a", near] = copies.start(own, xb(HERE, h, near, cols), af)
            got["b", near, HERE] = copies.start(own, xb(near, h, HERE, cols), bf)
        for i in (2 * h, 2 * h + 1):
            _, cols, _, near, next_, af, ab, bf, bb = streams[i]
            own, got = xb(HERE, h, HERE, cols), gather[i]
            got["a", next_] = copies.start(own, xb(HERE, h, next_, cols), ab)
            got["b", next_, HERE] = copies.start(own, xb(next_, h, HERE, cols), bb)

    def sx(dz, c):
        return shx.at[pl.ds((c * 4 + dz) * TOK, TOK)]

    ring = [
        copies.start(sx(HERE, 0), sx(PREV, 0), zp),
        copies.start(sx(HERE, 0), sx(NEXT, 0), zm),
    ]
    to_twin = [copies.start(sx(HERE, 0), sx(HERE, 1), twin)]

    def part(ref, cols):
        return ref.at[:, cols]

    def along_b(i, a):
        h, cols, _, near, next_, af, ab, bf, bb = streams[i]
        gather[i]["b", near, a] = copies.start(xb(HERE, h, a, cols), xb(near, h, a, cols), bf)
        gather[i]["b", next_, a] = copies.start(xb(HERE, h, a, cols), xb(next_, h, a, cols), bb)

    def pass_b(i, a):
        h, cols, _, near, next_, af, ab, bf, bb = streams[i]
        gather[i]["b", near, a].wait_recv()
        gather[i]["b", FAR, a] = copies.start(xb(near, h, a, cols), xb(FAR, h, a, cols), bf)

    four = range(4)
    for i in four:
        h, cols, _, near, next_, af, ab, bf, bb = streams[i]
        gather[i]["a", near].wait_recv()
        gather[i]["a", FAR] = copies.start(xb(HERE, h, near, cols), xb(HERE, h, FAR, cols), af)
        along_b(i, near)
    for i in four:
        pass_b(i, HERE)
    for i in four:
        gather[i]["a", streams[i][4]].wait_recv()
        along_b(i, streams[i][4])
    for i in four:
        gather[i]["a", FAR].wait_recv()
        along_b(i, FAR)

    def routed(start, rows):
        at = pl.ds(start, rows)
        gate = xs[at, D:].astype(F32)
        for k in range(3):
            both = jnp.dot(xs[at, 0:D], wgu[k], preferred_element_type=F32)
            value = jax.nn.silu(both[:, :128]) * both[:, 128:] * gate[:, k : k + 1]
            hid[0:rows, k * 128 : (k + 1) * 128] = value.astype(BF16)

        @pl.loop(0, D // 512)
        def _(n):
            cols = pl.ds(pl.multiple_of(n * 512, 512), 512)
            ys[at, cols] = jnp.dot(
                hid[0:rows, :], wd[:, cols], preferred_element_type=F32
            ).astype(BF16)

    for copy in load_routed:
        copy.wait()
    routed(row(HERE, 0, 0), 8 * HALF)
    for i in four:
        pass_b(i, streams[i][3])
    ring[0].wait_recv()
    ring.append(copies.start(part(sx(PREV, 0), lo), part(sx(FAR, 0), lo), zp))
    to_twin.append(copies.start(sx(PREV, 0), sx(PREV, 1), twin))
    ring[1].wait_recv()
    ring.append(copies.start(part(sx(NEXT, 0), hi), part(sx(FAR, 0), hi), zm))
    to_twin.append(copies.start(sx(NEXT, 0), sx(NEXT, 1), twin))
    for i in four:
        pass_b(i, streams[i][4])
    for i in four:
        pass_b(i, FAR)

    for copy in load_shared:
        copy.wait()

    def shared(c):
        @pl.loop(0, 2)
        def _(i):
            at = pl.ds(pl.multiple_of(c * 4 * TOK + i * 2 * TOK, 2 * TOK), 2 * TOK)
            both = jnp.dot(shx[at, :], sgu[...], preferred_element_type=F32)
            shh[...] = (jax.nn.silu(both[:, :SH]) * both[:, SH:]).astype(BF16)

            @pl.loop(0, D // 512)
            def _(n):
                cols = pl.ds(pl.multiple_of(n * 512, 512), 512)
                shp[at, cols] = lax.dot_general(
                    shh[...], sd[cols, :], (((1,), (1,)), ((), ())), preferred_element_type=F32
                ).astype(BF16)

    ring[2].wait_recv()
    ring[3].wait_recv()
    to_twin.append(copies.start(sx(FAR, 0), sx(FAR, 1), twin))
    for copy in to_twin:
        copy.wait_recv()
    shared(1)
    sums = [
        copies.start(shp.at[pl.ds((4 + dz) * TOK, TOK)], sib.at[pl.ds(dz * TOK, TOK)], twin)
        for dz in range(4)
    ]

    groups = ((1, PREV), (0, HERE))

    def yb(b, h, a, n, cols):
        return ys.at[pl.ds(row(b, h, a), n * HALF), cols]

    def spot(g):
        return pl.ds(2 * g * HALF, 2 * HALF)

    reduce = [{} for _ in streams]

    def direct(i):
        h, _, cols, near, next_, af, ab, bf, bb = streams[i]
        for g, a in groups:
            reduce[i]["behind", g] = copies.start(
                yb(near, h, a, 2, cols), behind.at[h, spot(g), cols], bb
            )

    for b in (PREV, NEXT):
        for i in four:
            if b != streams[i][3]:
                for a in four:
                    gather[i]["b", b, a].wait_recv()
        routed(row(b, 0, 0), 8 * HALF)
        for i in four:
            if streams[i][3] == b:
                direct(i)
    shared(0)
    for h in range(2):
        for i in (2 * h, 2 * h + 1):
            for a in four:
                gather[i]["b", FAR, a].wait_recv()
        routed(row(FAR, h, 0), 4 * HALF)
        for g, a in groups:
            for i in (2 * h, 2 * h + 1):
                _, _, cols, near, next_, af, ab, bf, bb = streams[i]
                reduce[i]["far", g] = copies.start(
                    yb(FAR, h, a, 2, cols), r1.at[h, spot(g), cols], bf
                )

    every = pl.ds(0, D)
    for copy in sums:
        copy.wait_recv()
    add_rows(shp, 0, 4 * TOK, every, [(sib, 0)])

    def sp(dz):
        return shp.at[pl.ds(dz * TOK, TOK)]

    zs = [
        copies.start(part(sp(FAR), lo), part(u1, lo), zp),
        copies.start(part(sp(FAR), hi), part(u1, hi), zm),
    ]

    for g, a in groups:
        for i in four:
            h, _, cols, near, next_, af, ab, bf, bb = streams[i]
            reduce[i]["far", g].wait_recv()
            add_rows(ys, row(next_, h, a), 2 * HALF, cols, [(r1.at[h], 2 * g * HALF)])
            reduce[i]["ahead", g] = copies.start(
                yb(next_, h, a, 2, cols), ahead.at[h, spot(g), cols], bf
            )
    zs[0].wait_recv()
    add_rows(shp, NEXT * TOK, TOK, lo, [(u1, 0)])
    zs.append(copies.start(sp(NEXT), u2.at[0], zp))
    zs[1].wait_recv()
    add_rows(shp, PREV * TOK, TOK, hi, [(u1, 0)])
    zs.append(copies.start(sp(PREV), u2.at[1], zm))

    def pass_a(i):
        h, _, cols, near, next_, af, ab, bf, bb = streams[i]
        reduce[i]["a far"].wait_recv()
        add_rows(ys, row(HERE, h, next_), HALF, cols, [(t1.at[h], 0)])
        reduce[i]["a ahead"] = copies.start(
            yb(HERE, h, next_, 1, cols), tahead.at[h, :, cols], af
        )

    for g, a in groups:
        for i in four:
            h, _, cols, near, next_, af, ab, bf, bb = streams[i]
            reduce[i]["behind", g].wait_recv()
            reduce[i]["ahead", g].wait_recv()
            add_rows(
                ys,
                row(HERE, h, a),
                2 * HALF,
                cols,
                [(ahead.at[h], 2 * g * HALF), (behind.at[h], 2 * g * HALF)],
            )
            if g == 1:
                reduce[i]["a far"] = copies.start(
                    yb(HERE, h, FAR, 1, cols), t1.at[h, :, cols], af
                )
            if near in (a, a + 1):
                reduce[i]["a behind"] = copies.start(
                    yb(HERE, h, near, 1, cols), tbehind.at[h, :, cols], ab
                )
    home = []
    for i in four:
        pass_a(i)
    for h in range(2):
        for i in (2 * h, 2 * h + 1):
            reduce[i]["a behind"].wait_recv()
            reduce[i]["a ahead"].wait_recv()
        first = row(HERE, h, HERE)
        add_rows(ys, first, HALF, every, [(tahead.at[h], 0), (tbehind.at[h], 0)])
        rows = slice(h * 64, h * 64 + 64)
        for g in range(3):
            cols = slice(g * TAIL, (g + 1) * TAIL)
            back[rows, cols] = (
                jnp.dot(spread, ys[first : first + HALF, cols], preferred_element_type=F32)
                + jnp.dot(
                    spread_tail[g], ys[first : first + HALF, MAIN:], preferred_element_type=F32
                )
            ).astype(BF16)
        for p in range(4 * h, 4 * h + 4):
            piece = pl.ds(p * PIECE, PIECE)
            if p:
                home.append(copies.start(back.at[piece], ret.at[piece], ep_from[ORDER[p]]))
            else:
                ret[piece, :] = back[piece, :]

    for copy in zs[2:]:
        copy.wait_recv()
    for copy in home:
        copy.wait_recv()
    over = (((0,), (0,)), ((), ()))
    for n in range(4):
        cols = slice(n * TAIL, (n + 1) * TAIL)
        if n < 3:
            total = lax.dot_general(place, ret[:, cols], over, preferred_element_type=F32)
        else:
            total = jnp.zeros((TOK, TAIL), F32)
            for g in range(3):
                total += lax.dot_general(
                    place_tail[g],
                    ret[:, g * TAIL : (g + 1) * TAIL],
                    over,
                    preferred_element_type=F32,
                )
        total += shp[0:TOK, cols].astype(F32)
        total += u2[0, :, cols].astype(F32) + u2[1, :, cols].astype(F32)
        out_ref[:, cols] = total.astype(BF16)

    for copy in copies.made:
        copy.wait_send()


def local(
    tokens,
    expert_ids,
    devices,
    slots,
    gates,
    w_gate,
    w_up,
    w_down,
    shared_gate,
    shared_up,
    shared_down,
):
    vmem = pl.BlockSpec(memory_space=pltpu.VMEM)
    anywhere = pl.BlockSpec(memory_space=pl.ANY)
    copies = 7 + 60 + 4 + 4 + 36 + 4 + 4 + 7
    return pl.pallas_call(
        kernel,
        out_shape=jax.ShapeDtypeStruct((TOK, D), BF16),
        in_specs=[vmem] * 4 + [anywhere] * 7,
        out_specs=vmem,
        scratch_shapes=[
            pltpu.VMEM((3, D, 256), BF16),
            pltpu.VMEM((384, D), BF16),
            pltpu.VMEM((D, 2 * SH), BF16),
            pltpu.VMEM((D, SH), BF16),
            pltpu.VMEM((TOK, MAIN + 128), BF16),
            pltpu.VMEM((TOK, MAIN + 128), BF16),
            pltpu.VMEM((32 * HALF, WIDE), BF16),
            pltpu.VMEM((32 * HALF, D), BF16),
            pltpu.VMEM((8 * HALF, 384), BF16),
            pltpu.VMEM((2, 4 * HALF, D), BF16),
            pltpu.VMEM((2, 4 * HALF, D), BF16),
            pltpu.VMEM((2, 4 * HALF, D), BF16),
            pltpu.VMEM((2, HALF, D), BF16),
            pltpu.VMEM((2, HALF, D), BF16),
            pltpu.VMEM((2, HALF, D), BF16),
            pltpu.VMEM((TOK, MAIN), BF16),
            pltpu.VMEM((TOK, MAIN), BF16),
            pltpu.VMEM((8 * TOK, D), BF16),
            pltpu.VMEM((8 * TOK, D), BF16),
            pltpu.VMEM((2 * TOK, SH), BF16),
            pltpu.VMEM((4 * TOK, D), BF16),
            pltpu.VMEM((TOK, D), BF16),
            pltpu.VMEM((2, TOK, D), BF16),
            pltpu.SemaphoreType.DMA((copies,)),
            pltpu.SemaphoreType.DMA((copies,)),
            pltpu.SemaphoreType.DMA((16,)),
        ],
        compiler_params=pltpu.CompilerParams(
            collective_id=0, has_side_effects=True, vmem_limit_bytes=62 * 1024 * 1024
        ),
        cost_estimate=pl.CostEstimate(
            flops=13_100_000_000, bytes_accessed=12_000_000, transcendentals=900_000
        ),
    )(
        expert_ids.T,
        devices.T,
        slots.T,
        gates.T,
        tokens,
        w_gate,
        w_up,
        w_down,
        shared_gate,
        shared_up,
        shared_down,
    )


def solution(mesh):
    in_specs = (
        P(("seq", "ep"), None),
        P(("seq", "ep"), None),
        P(("seq", "ep"), None),
        P(("seq", "ep"), None),
        P(("seq", "ep"), None),
        P("ep", None, "seq"),
        P("ep", None, "seq"),
        P("ep", "seq", None),
        P(None, "ep"),
        P(None, "ep"),
        P(None, "ep"),
    )
    out_specs = P(("seq", "ep"), None)
    return jax.shard_map(local, mesh=mesh, in_specs=in_specs, out_specs=out_specs, check_vma=False)
```

```python
import functools

import jax
import jax.numpy as jnp
from jax import lax
from jax.experimental import pallas as pl
from jax.experimental.pallas import tpu as pltpu
from jax.sharding import PartitionSpec as P

MESH = pl.DeviceIdType.MESH
F32 = jnp.float32
BF16 = jnp.bfloat16

SIDE = 4
N_EP = 8
TOK = 128
D = 2560
CAP = 12
PIECE = 16
HALF = 4 * CAP
SH = 256
LEFT = 1280
MAIN = 1920
TAIL = D - MAIN
ORDER = (0, 1, 2, 7, 6, 3, 4, 5)

HERE, NEXT, PREV, FAR = 0, 1, 2, 3


class Copies:
    def __init__(self, send, recv):
        self.send, self.recv, self.made = send, recv, []

    def start(self, src, dst, device):
        i = len(self.made)
        copy = pltpu.make_async_remote_copy(
            src_ref=src,
            dst_ref=dst,
            send_sem=self.send.at[i],
            recv_sem=self.recv.at[i],
            device_id=device,
            device_id_type=MESH,
        )
        copy.start()
        self.made.append(copy)
        return copy


def add_rows(dst, start, rows, cols, terms):
    step = 48 if rows % 48 == 0 else 32

    @pl.loop(0, rows // step)
    def _(i):
        at = pl.ds(pl.multiple_of(start + i * step, 16), step)
        total = dst[at, cols].astype(F32)
        for ref, first in terms:
            total += ref[pl.ds(pl.multiple_of(first + i * step, 16), step), cols].astype(F32)
        dst[at, cols] = total.astype(BF16)


def row(b, h, a):
    pair = a // 2
    return (((pair * 4 + (b + pair) % 4) * 2 + h) * 2 + a % 2) * HALF


def kernel(
    ids_ref,
    dev_ref,
    slot_ref,
    gates_ref,
    tok_hbm,
    wg_hbm,
    wu_hbm,
    wd_hbm,
    sg_hbm,
    su_hbm,
    sd_hbm,
    out_ref,
    wgu,
    wd,
    sgu,
    sd,
    send,
    land,
    gates_all,
    gate_cols,
    xs,
    ys,
    hid,
    r1,
    ahead,
    behind,
    t1,
    tahead,
    tbehind,
    back,
    ret,
    shx,
    shp,
    shh,
    sib,
    u1,
    u2,
    send_sem,
    recv_sem,
    local_sem,
):
    seq, ep = lax.axis_index("seq"), lax.axis_index("ep")
    y, x = seq // SIDE, lax.rem(seq, SIDE)
    z, core = ep // 2, lax.rem(ep, 2)

    def up(v, by):
        return lax.rem(v + by, SIDE)

    xp, xm = (y * SIDE + up(x, 1), ep), (y * SIDE + up(x, 3), ep)
    yp, ym = (up(y, 1) * SIDE + x, ep), (up(y, 3) * SIDE + x, ep)
    zp, zm = (seq, up(z, 1) * 2 + core), (seq, up(z, 3) * 2 + core)
    twin = (seq, z * 2 + 1 - core)
    ep_to = [(seq, lax.rem(ep + r, N_EP)) for r in range(N_EP)]
    ep_from = [(seq, lax.rem(ep + N_EP - r, N_EP)) for r in range(N_EP)]
    rings = [((xp, xm), (yp, ym)), ((yp, ym), (xp, xm))]
    xf, yf = (y * SIDE + up(x, 2), ep), (up(y, 2) * SIDE + x, ep)

    barrier = pltpu.get_barrier_semaphore()
    partners = [xp, xm, xf, yp, ym, yf] + ep_to[1:]
    for device in partners:
        pl.semaphore_signal(barrier, inc=1, device_id=device, device_id_type=MESH)

    loads = []

    def load(src, dst):
        copy = pltpu.make_async_copy(src, dst, local_sem.at[len(loads)])
        copy.start()
        loads.append(copy)
        return copy

    tok = shx.at[pl.ds(0, TOK)]
    load_tok = load(tok_hbm, tok)
    load_routed = []
    for k in range(3):
        load_routed.append(load(wg_hbm.at[k], wgu.at[k, :, pl.ds(0, 128)]))
        load_routed.append(load(wu_hbm.at[k], wgu.at[k, :, pl.ds(128, 128)]))
        load_routed.append(load(wd_hbm.at[k], wd.at[pl.ds(k * 128, 128)]))
    load_shared = [
        load(sg_hbm, sgu.at[:, pl.ds(0, SH)]),
        load(su_hbm, sgu.at[:, pl.ds(SH, SH)]),
        load(sd_hbm, sd),
    ]

    rows_i = lax.broadcasted_iota(jnp.int32, (TOK, TOK), 0)
    lanes_i = lax.broadcasted_iota(jnp.int32, (TOK, TOK), 1)
    place = jnp.zeros((TOK, TOK), F32)
    place_tail = [jnp.zeros((TOK, TOK), F32) for _ in range(3)]
    gate_of = [jnp.zeros((TOK, TOK), F32) for _ in range(3)]
    for j in range(3):
        dev = dev_ref[j : j + 1, :]
        slot = slot_ref[j : j + 1, :]
        turn = dev - ep
        turn = jnp.where(turn < 0, turn + N_EP, turn)
        piece = jnp.where(turn < 3, turn, jnp.where(turn < 6, turn + 2, 10 - turn))
        hit = rows_i == jnp.where(slot >= 0, piece * PIECE + slot, -1)
        place = jnp.where(hit, 1.0, place)
        for g in range(3):
            mine = (slot >= 4 * g) & (slot < 4 * g + 4)
            tail_row = jnp.where(mine, piece * PIECE + CAP - 4 * g + slot, -1)
            place_tail[g] = jnp.where(rows_i == tail_row, 1.0, place_tail[g])
        for k in range(3):
            summed = jnp.zeros((1, TOK), F32)
            for r in range(6):
                summed += jnp.where(
                    ids_ref[r : r + 1, :] == dev * 3 + k, gates_ref[r : r + 1, :], 0.0
                )
            gate_of[k] = jnp.where(hit, summed, gate_of[k])
    place = place.astype(BF16)
    place_tail = [p.astype(BF16) for p in place_tail]
    columns = jnp.zeros((TOK, TOK), F32)
    for k in range(3):
        column = jnp.sum(gate_of[k], axis=1, keepdims=True)
        columns = jnp.where(lanes_i == k, column, columns)
    send[:, MAIN:] = columns.astype(BF16)

    load_tok.wait()
    for g in range(3):
        cols = slice(g * TAIL, (g + 1) * TAIL)
        send[:, cols] = (
            jnp.dot(place, shx[0:TOK, cols], preferred_element_type=F32)
            + jnp.dot(place_tail[g], shx[0:TOK, MAIN:], preferred_element_type=F32)
        ).astype(BF16)

    pl.semaphore_wait(barrier, len(partners))
    copies = Copies(send_sem, recv_sem)

    def sx(dz, c):
        return shx.at[pl.ds((dz * 2 + c) * TOK, TOK)]

    arrive = [None]
    for p in range(1, N_EP):
        piece = pl.ds(p * PIECE, PIECE)
        arrive.append(copies.start(send.at[piece], land.at[piece], ep_to[ORDER[p]]))
    land[0:PIECE, :] = send[0:PIECE, :]
    to_twin = [copies.start(sx(HERE, 0), sx(HERE, 1), twin)]

    def dense(flip, g=None):
        shape = (4 * PIECE, HALF) if flip else (HALF, 4 * PIECE)
        one = lax.broadcasted_iota(jnp.int32, shape, 1 if flip else 0)
        two = lax.broadcasted_iota(jnp.int32, shape, 0 if flip else 1)
        hit = jnp.zeros(shape, F32)
        for i in range(4):
            first, count, shift = CAP * i, CAP, (PIECE - CAP) * i
            if g is not None:
                first, count, shift = first + 4 * g, 4, shift + CAP - 4 * g
            inside = (one >= first) & (one < first + count) & (two == one + shift)
            hit = jnp.where(inside, 1.0, hit)
        return hit.astype(BF16)

    squeeze, squeeze_tail = dense(False), [dense(False, g) for g in range(3)]
    spread, spread_tail = dense(True), [dense(True, g) for g in range(3)]

    lo, hi = pl.ds(0, LEFT), pl.ds(LEFT, D - LEFT)

    def xb(b, h, a, cols):
        return xs.at[pl.ds(row(b, h, a), HALF), cols]

    streams = []
    for h in range(2):
        (ap, am), (bp, bm) = rings[h]
        streams.append((h, lo, PREV, NEXT, ap, am, bp, bm))
        streams.append((h, hi, NEXT, PREV, am, ap, bm, bp))

    gather = [{} for _ in streams]
    for h in range(2):
        for p in range(4 * h, 4 * h + 4):
            if p:
                arrive[p].wait_recv()
        first = row(HERE, h, HERE)
        rows = slice(h * 64, h * 64 + 64)
        for g in range(3):
            cols = slice(g * TAIL, (g + 1) * TAIL)
            xs[first : first + HALF, cols] = jnp.dot(
                squeeze, land[rows, cols], preferred_element_type=F32
            ).astype(BF16)
        tail = jnp.zeros((HALF, TAIL), F32)
        for g in range(3):
            cols = slice(g * TAIL, (g + 1) * TAIL)
            tail += jnp.dot(squeeze_tail[g], land[rows, cols], preferred_element_type=F32)
        xs[first : first + HALF, MAIN:D] = tail.astype(BF16)
        for i in (2 * h, 2 * h + 1):
            _, cols, near, next_, af, ab, bf, bb = streams[i]
            own, got = xb(HERE, h, HERE, cols), gather[i]
            got["a", near] = copies.start(own, xb(HERE, h, near, cols), af)
            got["b", near, HERE] = copies.start(own, xb(near, h, HERE, cols), bf)
        for i in (2 * h, 2 * h + 1):
            _, cols, near, next_, af, ab, bf, bb = streams[i]
            own, got = xb(HERE, h, HERE, cols), gather[i]
            got["a", next_] = copies.start(own, xb(HERE, h, next_, cols), ab)
            got["b", next_, HERE] = copies.start(own, xb(next_, h, HERE, cols), bb)

    lands = lax.broadcasted_iota(jnp.int32, (TOK, TOK), 0)
    slots_i = lax.broadcasted_iota(jnp.int32, (TOK, TOK), 1)
    which = jnp.zeros((TOK, TOK), F32)
    for p in range(N_EP):
        inside = (slots_i >= CAP * p) & (slots_i < CAP * (p + 1))
        which = jnp.where(inside & (lands == slots_i + (PIECE - CAP) * p), 1.0, which)
    turned = lax.dot_general(
        land[:, MAIN:],
        which.astype(BF16),
        (((0,), (0,)), ((), ())),
        preferred_element_type=F32,
    )
    gates_all[0:16, :] = turned[0:16, :].astype(BF16)

    def tiles(ry, rx, n):
        return gates_all.at[pl.ds((ry * 4 + rx) * 16, n * 16)]

    gate_copies = [
        copies.start(tiles(HERE, HERE, 1), tiles(HERE, PREV, 1), xp),
        copies.start(tiles(HERE, HERE, 1), tiles(HERE, NEXT, 1), xm),
        copies.start(tiles(HERE, HERE, 1), tiles(HERE, FAR, 1), xf),
    ]

    ring = [
        copies.start(sx(HERE, 0), sx(PREV, 0), zp),
        copies.start(sx(HERE, 0), sx(NEXT, 0), zm),
    ]

    def part(ref, cols):
        return ref.at[:, cols]

    def along_b(i, a):
        h, cols, near, next_, af, ab, bf, bb = streams[i]
        gather[i]["b", near, a] = copies.start(xb(HERE, h, a, cols), xb(near, h, a, cols), bf)
        gather[i]["b", next_, a] = copies.start(xb(HERE, h, a, cols), xb(next_, h, a, cols), bb)

    def pass_b(i, a):
        h, cols, near, next_, af, ab, bf, bb = streams[i]
        gather[i]["b", near, a].wait_recv()
        gather[i]["b", FAR, a] = copies.start(xb(near, h, a, cols), xb(FAR, h, a, cols), bf)

    sums = {}

    def shared(dz):
        at = pl.ds(dz * 2 * TOK, 2 * TOK)
        both = jnp.dot(shx[at, :], sgu[...], preferred_element_type=F32)
        shh[...] = (jax.nn.silu(both[:, :SH]) * both[:, SH:]).astype(BF16)

        @pl.loop(0, D // 512)
        def _(n):
            cols = pl.ds(pl.multiple_of(n * 512, 512), 512)
            shp[at, cols] = lax.dot_general(
                shh[...], sd[cols, :], (((1,), (1,)), ((), ())), preferred_element_type=F32
            ).astype(BF16)

        sums[dz] = copies.start(
            shp.at[pl.ds((dz * 2 + 1) * TOK, TOK)], sib.at[pl.ds(dz * TOK, TOK)], twin
        )

    for copy in load_shared:
        copy.wait()
    to_twin[0].wait_recv()
    shared(HERE)

    four = range(4)
    for i in four:
        h, cols, near, next_, af, ab, bf, bb = streams[i]
        gather[i]["a", near].wait_recv()
        gather[i]["a", FAR] = copies.start(xb(HERE, h, near, cols), xb(HERE, h, FAR, cols), af)
        along_b(i, near)
    for i in four:
        pass_b(i, HERE)
    for i in four:
        gather[i]["a", streams[i][3]].wait_recv()
        along_b(i, streams[i][3])
    for copy in gate_copies[:3]:
        copy.wait_recv()
    gate_copies += [
        copies.start(tiles(HERE, HERE, 4), tiles(PREV, HERE, 4), yp),
        copies.start(tiles(HERE, HERE, 4), tiles(NEXT, HERE, 4), ym),
        copies.start(tiles(HERE, HERE, 4), tiles(FAR, HERE, 4), yf),
    ]
    for i in four:
        gather[i]["a", FAR].wait_recv()
        along_b(i, FAR)

    def experts(start, rows):
        spots = {row(b, h, a): (h, a, b) for b in four for h in range(2) for a in four}
        columns = []
        for first in range(start, start + rows, HALF):
            h, a, b = spots[first]
            columns.append((h, (b * 4 + a if h == 0 else a * 4 + b) * 16))
        at = pl.ds(start, rows)
        for k in range(3):
            both = jnp.dot(xs[at, :], wgu[k], preferred_element_type=F32)
            gate = jnp.concatenate([gate_cols[h, :, c + k : c + k + 1] for h, c in columns], 0)
            value = jax.nn.silu(both[:, :128]) * both[:, 128:] * gate
            hid[0:rows, k * 128 : (k + 1) * 128] = value.astype(BF16)

    def down(start, rows, cols):
        ys[pl.ds(start, rows), cols] = jnp.dot(
            hid[0:rows, :], wd[:, cols], preferred_element_type=F32
        ).astype(BF16)

    def routed(start, rows):
        experts(start, rows)

        @pl.loop(0, D // 512)
        def _(n):
            down(start, rows, pl.ds(pl.multiple_of(n * 512, 512), 512))

    for i in four:
        pass_b(i, streams[i][2])
    for i in four:
        pass_b(i, streams[i][3])
    ring[0].wait_recv()
    ring.append(copies.start(part(sx(PREV, 0), lo), part(sx(FAR, 0), lo), zp))
    to_twin.append(copies.start(sx(PREV, 0), sx(PREV, 1), twin))
    ring[1].wait_recv()
    ring.append(copies.start(part(sx(NEXT, 0), hi), part(sx(FAR, 0), hi), zm))
    to_twin.append(copies.start(sx(NEXT, 0), sx(NEXT, 1), twin))
    for copy in load_routed:
        copy.wait()
    for copy in gate_copies[3:]:
        copy.wait_recv()
    for h in range(2):
        spots = lax.broadcasted_iota(jnp.int32, (HALF, TOK), 1) == (
            lax.broadcasted_iota(jnp.int32, (HALF, TOK), 0) + h * HALF
        )
        gate_cols[h] = lax.dot_general(
            jnp.where(spots, 1.0, 0.0).astype(BF16),
            gates_all[...],
            (((1,), (1,)), ((), ())),
            preferred_element_type=F32,
        )
    for a in (HERE, NEXT):
        for i in four:
            gather[i]["b", streams[i][3], a].wait_recv()
    routed(0, 12 * HALF)
    to_twin[1].wait_recv()
    to_twin[2].wait_recv()
    shared(PREV)
    shared(NEXT)
    for i in four:
        pass_b(i, FAR)
    ring[2].wait_recv()
    ring[3].wait_recv()
    to_twin.append(copies.start(sx(FAR, 0), sx(FAR, 1), twin))

    groups = ((1, PREV), (0, HERE))
    phases = ((pl.ds(0, TAIL), pl.ds(MAIN, TAIL)), (pl.ds(TAIL, TAIL), pl.ds(2 * TAIL, TAIL)))

    def yb(b, h, a, n, cols):
        return ys.at[pl.ds(row(b, h, a), n * HALF), cols]

    def spot(g):
        return pl.ds(2 * g * HALF, 2 * HALF)

    reduce = [{} for _ in streams]

    def direct(g, a):
        for i in four:
            h, cols, near, next_, af, ab, bf, bb = streams[i]
            reduce[i]["behind", g] = copies.start(
                yb(near, h, a, 2, cols), behind.at[h, spot(g), cols], bb
            )

    direct(0, HERE)
    for a in (PREV, FAR):
        for i in four:
            gather[i]["b", streams[i][3], a].wait_recv()
    routed(20 * HALF, 12 * HALF)
    direct(1, PREV)
    to_twin[3].wait_recv()
    shared(FAR)
    for i in four:
        for a in four:
            gather[i]["b", FAR, a].wait_recv()
    experts(12 * HALF, 8 * HALF)
    for q in range(2):
        for cols in phases[q]:
            down(12 * HALF, 8 * HALF, cols)
        for g, a in groups:
            for i in four:
                h, _, near, next_, af, ab, bf, bb = streams[i]
                cols = phases[q][i % 2]
                reduce[i]["far", q, g] = copies.start(
                    yb(FAR, h, a, 2, cols), r1.at[h, spot(g), cols], bf
                )

    def sp(dz):
        return shp.at[pl.ds(dz * 2 * TOK, TOK)]

    every = pl.ds(0, D)
    for dz in (FAR, NEXT, PREV, HERE):
        sums[dz].wait_recv()
        add_rows(shp, dz * 2 * TOK, TOK, every, [(sib, dz * TOK)])
        if dz == FAR:
            zs = [
                copies.start(part(sp(FAR), lo), part(u1, lo), zp),
                copies.start(part(sp(FAR), hi), part(u1, hi), zm),
            ]

    for q in range(2):
        for g, a in groups:
            for i in four:
                h, _, near, next_, af, ab, bf, bb = streams[i]
                cols = phases[q][i % 2]
                reduce[i]["far", q, g].wait_recv()
                add_rows(ys, row(next_, h, a), 2 * HALF, cols, [(r1.at[h], 2 * g * HALF)])
                reduce[i]["ahead", q, g] = copies.start(
                    yb(next_, h, a, 2, cols), ahead.at[h, spot(g), cols], bf
                )
    zs[0].wait_recv()
    add_rows(shp, NEXT * 2 * TOK, TOK, lo, [(u1, 0)])
    zs.append(copies.start(sp(NEXT), u2.at[0], zp))
    zs[1].wait_recv()
    add_rows(shp, PREV * 2 * TOK, TOK, hi, [(u1, 0)])
    zs.append(copies.start(sp(PREV), u2.at[1], zm))

    def end_b(q):
        for g, a in groups:
            for i in four:
                h, _, near, next_, af, ab, bf, bb = streams[i]
                cols = phases[q][i % 2]
                if q == 0:
                    reduce[i]["behind", g].wait_recv()
                reduce[i]["ahead", q, g].wait_recv()
                add_rows(
                    ys,
                    row(HERE, h, a),
                    2 * HALF,
                    cols,
                    [(ahead.at[h], 2 * g * HALF), (behind.at[h], 2 * g * HALF)],
                )
                if g == 1:
                    reduce[i]["a far", q] = copies.start(
                        yb(HERE, h, FAR, 1, cols), t1.at[h, :, cols], af
                    )
                if near in (a, a + 1):
                    reduce[i]["a behind", q] = copies.start(
                        yb(HERE, h, near, 1, cols), tbehind.at[h, :, cols], ab
                    )

    def pass_a(q):
        for i in four:
            h, _, near, next_, af, ab, bf, bb = streams[i]
            cols = phases[q][i % 2]
            reduce[i]["a far", q].wait_recv()
            add_rows(ys, row(HERE, h, next_), HALF, cols, [(t1.at[h], 0)])
            reduce[i]["a ahead", q] = copies.start(
                yb(HERE, h, next_, 1, cols), tahead.at[h, :, cols], af
            )

    home = []

    def end_a(q):
        for h in range(2):
            first = row(HERE, h, HERE)
            for i in (2 * h, 2 * h + 1):
                reduce[i]["a behind", q].wait_recv()
                reduce[i]["a ahead", q].wait_recv()
                cols = phases[q][i % 2]
                add_rows(ys, first, HALF, cols, [(tahead.at[h], 0), (tbehind.at[h], 0)])
            rows = slice(h * 64, h * 64 + 64)
            for g in ((0,), (1, 2))[q]:
                cols = slice(g * TAIL, (g + 1) * TAIL)
                back[rows, cols] = (
                    jnp.dot(spread, ys[first : first + HALF, cols], preferred_element_type=F32)
                    + jnp.dot(
                        spread_tail[g], ys[first : first + HALF, MAIN:], preferred_element_type=F32
                    )
                ).astype(BF16)
            cols = (pl.ds(0, TAIL), pl.ds(TAIL, 2 * TAIL))[q]
            for p in range(4 * h, 4 * h + 4):
                piece = pl.ds(p * PIECE, PIECE)
                if p:
                    home.append(
                        copies.start(back.at[piece, cols], ret.at[piece, cols], ep_from[ORDER[p]])
                    )
                else:
                    ret[piece, cols] = back[piece, cols]

    end_b(0)
    pass_a(0)
    end_b(1)
    end_a(0)
    pass_a(1)
    end_a(1)

    for copy in zs[2:]:
        copy.wait_recv()
    for copy in home:
        copy.wait_recv()
    over = (((0,), (0,)), ((), ()))
    for n in range(4):
        cols = slice(n * TAIL, (n + 1) * TAIL)
        if n < 3:
            total = lax.dot_general(place, ret[:, cols], over, preferred_element_type=F32)
        else:
            total = jnp.zeros((TOK, TAIL), F32)
            for g in range(3):
                total += lax.dot_general(
                    place_tail[g],
                    ret[:, g * TAIL : (g + 1) * TAIL],
                    over,
                    preferred_element_type=F32,
                )
        total += shp[0:TOK, cols].astype(F32)
        total += u2[0, :, cols].astype(F32) + u2[1, :, cols].astype(F32)
        out_ref[:, cols] = total.astype(BF16)

    for copy in copies.made:
        copy.wait_send()


def local(
    tokens,
    expert_ids,
    devices,
    slots,
    gates,
    w_gate,
    w_up,
    w_down,
    shared_gate,
    shared_up,
    shared_down,
):
    vmem = pl.BlockSpec(memory_space=pltpu.VMEM)
    anywhere = pl.BlockSpec(memory_space=pl.ANY)
    copies = 7 + 60 + 6 + 4 + 4 + 64 + 4 + 4 + 14
    return pl.pallas_call(
        kernel,
        out_shape=jax.ShapeDtypeStruct((TOK, D), BF16),
        in_specs=[vmem] * 4 + [anywhere] * 7,
        out_specs=vmem,
        scratch_shapes=[
            pltpu.VMEM((3, D, 256), BF16),
            pltpu.VMEM((384, D), BF16),
            pltpu.VMEM((D, 2 * SH), BF16),
            pltpu.VMEM((D, SH), BF16),
            pltpu.VMEM((TOK, MAIN + 128), BF16),
            pltpu.VMEM((TOK, MAIN + 128), BF16),
            pltpu.VMEM((256, 128), BF16),
            pltpu.VMEM((2, HALF, 256), F32),
            pltpu.VMEM((32 * HALF, D), BF16),
            pltpu.VMEM((32 * HALF, D), BF16),
            pltpu.VMEM((12 * HALF, 384), BF16),
            pltpu.VMEM((2, 4 * HALF, D), BF16),
            pltpu.VMEM((2, 4 * HALF, D), BF16),
            pltpu.VMEM((2, 4 * HALF, D), BF16),
            pltpu.VMEM((2, HALF, D), BF16),
            pltpu.VMEM((2, HALF, D), BF16),
            pltpu.VMEM((2, HALF, D), BF16),
            pltpu.VMEM((TOK, MAIN), BF16),
            pltpu.VMEM((TOK, MAIN), BF16),
            pltpu.VMEM((8 * TOK, D), BF16),
            pltpu.VMEM((8 * TOK, D), BF16),
            pltpu.VMEM((2 * TOK, SH), BF16),
            pltpu.VMEM((4 * TOK, D), BF16),
            pltpu.VMEM((TOK, D), BF16),
            pltpu.VMEM((2, TOK, D), BF16),
            pltpu.SemaphoreType.DMA((copies,)),
            pltpu.SemaphoreType.DMA((copies,)),
            pltpu.SemaphoreType.DMA((16,)),
        ],
        compiler_params=pltpu.CompilerParams(
            collective_id=0, has_side_effects=True, vmem_limit_bytes=62 * 1024 * 1024
        ),
        cost_estimate=pl.CostEstimate(
            flops=13_100_000_000, bytes_accessed=12_000_000, transcendentals=900_000
        ),
    )(
        expert_ids.T,
        devices.T,
        slots.T,
        gates.T,
        tokens,
        w_gate,
        w_up,
        w_down,
        shared_gate,
        shared_up,
        shared_down,
    )


def solution(mesh):
    in_specs = (
        P(("seq", "ep"), None),
        P(("seq", "ep"), None),
        P(("seq", "ep"), None),
        P(("seq", "ep"), None),
        P(("seq", "ep"), None),
        P("ep", None, "seq"),
        P("ep", None, "seq"),
        P("ep", "seq", None),
        P(None, "ep"),
        P(None, "ep"),
        P(None, "ep"),
    )
    out_specs = P(("seq", "ep"), None)
    return jax.shard_map(local, mesh=mesh, in_specs=in_specs, out_specs=out_specs, check_vma=False)
```

```python
import functools

import jax
import jax.numpy as jnp
from jax import lax
from jax.experimental import pallas as pl
from jax.experimental.pallas import tpu as pltpu
from jax.sharding import PartitionSpec as P

MESH = pl.DeviceIdType.MESH
F32 = jnp.float32
BF16 = jnp.bfloat16

SIDE = 4
N_EP = 8
TOK = 128
D = 2560
CAP = 12
PIECE = 16
HALF = 4 * CAP
SH = 256
LEFT = 1280
MAIN = 1920
TAIL = D - MAIN
EARLY = 896
ORDER = (0, 1, 2, 7, 6, 3, 4, 5)

HERE, NEXT, PREV, FAR = 0, 1, 2, 3


class Copies:
    def __init__(self, send, recv):
        self.send, self.recv, self.made = send, recv, []

    def start(self, src, dst, device):
        i = len(self.made)
        copy = pltpu.make_async_remote_copy(
            src_ref=src,
            dst_ref=dst,
            send_sem=self.send.at[i],
            recv_sem=self.recv.at[i],
            device_id=device,
            device_id_type=MESH,
        )
        copy.start()
        self.made.append(copy)
        return copy


def add_rows(dst, start, rows, cols, terms):
    step = 48 if rows % 48 == 0 else 32

    @pl.loop(0, rows // step)
    def _(i):
        at = pl.ds(pl.multiple_of(start + i * step, 16), step)
        total = dst[at, cols].astype(F32)
        for ref, first in terms:
            total += ref[pl.ds(pl.multiple_of(first + i * step, 16), step), cols].astype(F32)
        dst[at, cols] = total.astype(BF16)


def row(b, h, a):
    pair = a // 2
    return (((pair * 4 + (b + pair) % 4) * 2 + h) * 2 + a % 2) * HALF


def kernel(
    ids_hbm,
    dev_hbm,
    slot_hbm,
    gates_hbm,
    tok_hbm,
    wg_hbm,
    wu_hbm,
    wd_hbm,
    sg_hbm,
    su_hbm,
    sd_hbm,
    out_hbm,
    ids_ref,
    dev_ref,
    slot_ref,
    gates_ref,
    out_ref,
    wgu,
    wd,
    sgu,
    sd,
    send,
    land,
    gates_all,
    gate_cols,
    xs,
    ys,
    hid,
    r1,
    ahead,
    behind,
    t1,
    tahead,
    tbehind,
    back,
    ret,
    shx,
    shp,
    shh,
    sib,
    u1,
    u2,
    send_sem,
    recv_sem,
    local_sem,
):
    seq, ep = lax.axis_index("seq"), lax.axis_index("ep")
    y, x = seq // SIDE, lax.rem(seq, SIDE)
    z, core = ep // 2, lax.rem(ep, 2)

    def up(v, by):
        return lax.rem(v + by, SIDE)

    xp, xm = (y * SIDE + up(x, 1), ep), (y * SIDE + up(x, 3), ep)
    yp, ym = (up(y, 1) * SIDE + x, ep), (up(y, 3) * SIDE + x, ep)
    zp, zm = (seq, up(z, 1) * 2 + core), (seq, up(z, 3) * 2 + core)
    twin = (seq, z * 2 + 1 - core)
    ep_to = [(seq, lax.rem(ep + r, N_EP)) for r in range(N_EP)]
    ep_from = [(seq, lax.rem(ep + N_EP - r, N_EP)) for r in range(N_EP)]
    rings = [((xp, xm), (yp, ym)), ((yp, ym), (xp, xm))]
    xf, yf = (y * SIDE + up(x, 2), ep), (up(y, 2) * SIDE + x, ep)

    barrier = pltpu.get_barrier_semaphore()
    partners = [xp, xm, xf, yp, ym, yf] + ep_to[1:]
    for device in partners:
        pl.semaphore_signal(barrier, inc=1, device_id=device, device_id_type=MESH)

    loads = []

    def load(src, dst):
        copy = pltpu.make_async_copy(src, dst, local_sem.at[len(loads)])
        copy.start()
        loads.append(copy)
        return copy

    tok = shx.at[pl.ds(0, TOK)]
    load_small = [
        load(ids_hbm, ids_ref),
        load(dev_hbm, dev_ref),
        load(slot_hbm, slot_ref),
        load(gates_hbm, gates_ref),
    ]
    load_tok = load(tok_hbm, tok)
    load_routed = []
    for k in range(3):
        load_routed.append(load(wg_hbm.at[k], wgu.at[k, :, pl.ds(0, 128)]))
        load_routed.append(load(wu_hbm.at[k], wgu.at[k, :, pl.ds(128, 128)]))
        load_routed.append(load(wd_hbm.at[k], wd.at[pl.ds(k * 128, 128)]))
    load_shared = [
        load(sg_hbm, sgu.at[:, pl.ds(0, SH)]),
        load(su_hbm, sgu.at[:, pl.ds(SH, SH)]),
        load(sd_hbm, sd),
    ]

    rows_i = lax.broadcasted_iota(jnp.int32, (TOK, TOK), 0)
    lanes_i = lax.broadcasted_iota(jnp.int32, (TOK, TOK), 1)
    for copy in load_small:
        copy.wait()
    place = jnp.zeros((TOK, TOK), F32)
    place_tail = [jnp.zeros((TOK, TOK), F32) for _ in range(3)]
    gate_of = [jnp.zeros((TOK, TOK), F32) for _ in range(3)]
    for j in range(3):
        dev = dev_ref[j : j + 1, :]
        slot = slot_ref[j : j + 1, :]
        turn = dev - ep
        turn = jnp.where(turn < 0, turn + N_EP, turn)
        piece = jnp.where(turn < 3, turn, jnp.where(turn < 6, turn + 2, 10 - turn))
        hit = rows_i == jnp.where(slot >= 0, piece * PIECE + slot, -1)
        place = jnp.where(hit, 1.0, place)
        for g in range(3):
            mine = (slot >= 4 * g) & (slot < 4 * g + 4)
            tail_row = jnp.where(mine, piece * PIECE + CAP - 4 * g + slot, -1)
            place_tail[g] = jnp.where(rows_i == tail_row, 1.0, place_tail[g])
        for k in range(3):
            summed = jnp.zeros((1, TOK), F32)
            for r in range(6):
                summed += jnp.where(
                    ids_ref[r : r + 1, :] == dev * 3 + k, gates_ref[r : r + 1, :], 0.0
                )
            gate_of[k] = jnp.where(hit, summed, gate_of[k])
    place = place.astype(BF16)
    place_tail = [p.astype(BF16) for p in place_tail]
    columns = jnp.zeros((TOK, TOK), F32)
    for k in range(3):
        column = jnp.sum(gate_of[k], axis=1, keepdims=True)
        columns = jnp.where(lanes_i == k, column, columns)
    send[:, MAIN:] = columns.astype(BF16)

    load_tok.wait()
    for g in range(3):
        cols = slice(g * TAIL, (g + 1) * TAIL)
        send[:, cols] = (
            jnp.dot(place, shx[0:TOK, cols], preferred_element_type=F32)
            + jnp.dot(place_tail[g], shx[0:TOK, MAIN:], preferred_element_type=F32)
        ).astype(BF16)

    pl.semaphore_wait(barrier, len(partners))
    copies = Copies(send_sem, recv_sem)

    def sx(dz, c):
        return shx.at[pl.ds((dz * 2 + c) * TOK, TOK)]

    arrive = [None]

    def exchange(first, end):
        for p in range(first, end):
            piece = pl.ds(p * PIECE, PIECE)
            arrive.append(copies.start(send.at[piece], land.at[piece], ep_to[ORDER[p]]))

    exchange(1, 4)
    land[0:PIECE, :] = send[0:PIECE, :]
    to_twin = [copies.start(sx(HERE, 0), sx(HERE, 1), twin)]

    def dense(flip, g=None):
        shape = (4 * PIECE, HALF) if flip else (HALF, 4 * PIECE)
        one = lax.broadcasted_iota(jnp.int32, shape, 1 if flip else 0)
        two = lax.broadcasted_iota(jnp.int32, shape, 0 if flip else 1)
        hit = jnp.zeros(shape, F32)
        for i in range(4):
            first, count, shift = CAP * i, CAP, (PIECE - CAP) * i
            if g is not None:
                first, count, shift = first + 4 * g, 4, shift + CAP - 4 * g
            inside = (one >= first) & (one < first + count) & (two == one + shift)
            hit = jnp.where(inside, 1.0, hit)
        return hit.astype(BF16)

    squeeze, squeeze_tail = dense(False), [dense(False, g) for g in range(3)]
    spread = dense(True)

    lo, hi = pl.ds(0, LEFT), pl.ds(LEFT, D - LEFT)

    def xb(b, h, a, cols):
        return xs.at[pl.ds(row(b, h, a), HALF), cols]

    streams = []
    for h in range(2):
        (ap, am), (bp, bm) = rings[h]
        streams.append((h, lo, PREV, NEXT, ap, am, bp, bm))
        streams.append((h, hi, NEXT, PREV, am, ap, bm, bp))

    gather = [{} for _ in streams]
    for h in range(2):
        for p in range(4 * h, 4 * h + 4):
            if p:
                arrive[p].wait_recv()
        if h == 0:
            exchange(4, 8)
        first = row(HERE, h, HERE)
        rows = slice(h * 64, h * 64 + 64)
        for g in range(3):
            cols = slice(g * TAIL, (g + 1) * TAIL)
            xs[first : first + HALF, cols] = jnp.dot(
                squeeze, land[rows, cols], preferred_element_type=F32
            ).astype(BF16)
        tail = jnp.zeros((HALF, TAIL), F32)
        for g in range(3):
            cols = slice(g * TAIL, (g + 1) * TAIL)
            tail += jnp.dot(squeeze_tail[g], land[rows, cols], preferred_element_type=F32)
        xs[first : first + HALF, MAIN:D] = tail.astype(BF16)
        for i in (2 * h, 2 * h + 1):
            _, cols, near, next_, af, ab, bf, bb = streams[i]
            own, got = xb(HERE, h, HERE, cols), gather[i]
            got["a", near] = copies.start(own, xb(HERE, h, near, cols), af)
            got["b", near, HERE] = copies.start(own, xb(near, h, HERE, cols), bf)
        for i in (2 * h, 2 * h + 1):
            _, cols, near, next_, af, ab, bf, bb = streams[i]
            own, got = xb(HERE, h, HERE, cols), gather[i]
            got["a", next_] = copies.start(own, xb(HERE, h, next_, cols), ab)
            got["b", next_, HERE] = copies.start(own, xb(next_, h, HERE, cols), bb)

    lands = lax.broadcasted_iota(jnp.int32, (TOK, TOK), 0)
    slots_i = lax.broadcasted_iota(jnp.int32, (TOK, TOK), 1)
    which = jnp.zeros((TOK, TOK), F32)
    for p in range(N_EP):
        inside = (slots_i >= CAP * p) & (slots_i < CAP * (p + 1))
        which = jnp.where(inside & (lands == slots_i + (PIECE - CAP) * p), 1.0, which)
    turned = lax.dot_general(
        land[:, MAIN:],
        which.astype(BF16),
        (((0,), (0,)), ((), ())),
        preferred_element_type=F32,
    )
    gates_all[0:16, :] = turned[0:16, :].astype(BF16)

    def tiles(ry, rx, n):
        return gates_all.at[pl.ds((ry * 4 + rx) * 16, n * 16)]

    gate_copies = [
        copies.start(tiles(HERE, HERE, 1), tiles(HERE, PREV, 1), xp),
        copies.start(tiles(HERE, HERE, 1), tiles(HERE, NEXT, 1), xm),
        copies.start(tiles(HERE, HERE, 1), tiles(HERE, FAR, 1), xf),
    ]

    ring = [
        copies.start(sx(HERE, 0), sx(PREV, 0), zp),
        copies.start(sx(HERE, 0), sx(NEXT, 0), zm),
    ]

    def part(ref, cols):
        return ref.at[:, cols]

    def along_b(i, a):
        h, cols, near, next_, af, ab, bf, bb = streams[i]
        gather[i]["b", near, a] = copies.start(xb(HERE, h, a, cols), xb(near, h, a, cols), bf)
        gather[i]["b", next_, a] = copies.start(xb(HERE, h, a, cols), xb(next_, h, a, cols), bb)

    def pass_b(i, a):
        h, cols, near, next_, af, ab, bf, bb = streams[i]
        gather[i]["b", near, a].wait_recv()
        gather[i]["b", FAR, a] = copies.start(xb(near, h, a, cols), xb(FAR, h, a, cols), bf)

    sums = {}

    def shared(dz):
        at = pl.ds(dz * 2 * TOK, 2 * TOK)
        both = jnp.dot(shx[at, :], sgu[...], preferred_element_type=F32)
        shh[...] = (jax.nn.silu(both[:, :SH]) * both[:, SH:]).astype(BF16)

        @pl.loop(0, D // 512)
        def _(n):
            cols = pl.ds(pl.multiple_of(n * 512, 512), 512)
            shp[at, cols] = lax.dot_general(
                shh[...], sd[cols, :], (((1,), (1,)), ((), ())), preferred_element_type=F32
            ).astype(BF16)

        sums[dz] = copies.start(
            shp.at[pl.ds((dz * 2 + 1) * TOK, TOK)], sib.at[pl.ds(dz * TOK, TOK)], twin
        )

    for copy in load_shared:
        copy.wait()
    to_twin[0].wait_recv()
    shared(HERE)

    four = range(4)
    for i in four:
        h, cols, near, next_, af, ab, bf, bb = streams[i]
        gather[i]["a", near].wait_recv()
        gather[i]["a", FAR] = copies.start(xb(HERE, h, near, cols), xb(HERE, h, FAR, cols), af)
        along_b(i, near)
    for i in four:
        pass_b(i, HERE)
    for i in four:
        gather[i]["a", streams[i][3]].wait_recv()
        along_b(i, streams[i][3])
    for copy in gate_copies[:3]:
        copy.wait_recv()
    gate_copies += [
        copies.start(tiles(HERE, HERE, 4), tiles(PREV, HERE, 4), yp),
        copies.start(tiles(HERE, HERE, 4), tiles(NEXT, HERE, 4), ym),
        copies.start(tiles(HERE, HERE, 4), tiles(FAR, HERE, 4), yf),
    ]
    for i in four:
        gather[i]["a", FAR].wait_recv()
        along_b(i, FAR)

    def experts(start, rows):
        spots = {row(b, h, a): (h, a, b) for b in four for h in range(2) for a in four}
        columns = []
        for first in range(start, start + rows, HALF):
            h, a, b = spots[first]
            columns.append((h, (b * 4 + a if h == 0 else a * 4 + b) * 16))
        at = pl.ds(start, rows)
        for k in range(3):
            both = jnp.dot(xs[at, :], wgu[k], preferred_element_type=F32)
            gate = jnp.concatenate([gate_cols[h, :, c + k : c + k + 1] for h, c in columns], 0)
            value = jax.nn.silu(both[:, :128]) * both[:, 128:] * gate
            hid[0:rows, k * 128 : (k + 1) * 128] = value.astype(BF16)

    def down(start, rows, cols):
        ys[pl.ds(start, rows), cols] = jnp.dot(
            hid[0:rows, :], wd[:, cols], preferred_element_type=F32
        ).astype(BF16)

    def routed(start, rows):
        experts(start, rows)

        @pl.loop(0, D // 512)
        def _(n):
            down(start, rows, pl.ds(pl.multiple_of(n * 512, 512), 512))

    for i in four:
        pass_b(i, streams[i][2])
    for i in four:
        pass_b(i, streams[i][3])
    ring[0].wait_recv()
    ring.append(copies.start(part(sx(PREV, 0), lo), part(sx(FAR, 0), lo), zp))
    to_twin.append(copies.start(sx(PREV, 0), sx(PREV, 1), twin))
    ring[1].wait_recv()
    ring.append(copies.start(part(sx(NEXT, 0), hi), part(sx(FAR, 0), hi), zm))
    to_twin.append(copies.start(sx(NEXT, 0), sx(NEXT, 1), twin))
    for copy in load_routed:
        copy.wait()
    for copy in gate_copies[3:]:
        copy.wait_recv()
    for h in range(2):
        spots = lax.broadcasted_iota(jnp.int32, (HALF, TOK), 1) == (
            lax.broadcasted_iota(jnp.int32, (HALF, TOK), 0) + h * HALF
        )
        gate_cols[h] = lax.dot_general(
            jnp.where(spots, 1.0, 0.0).astype(BF16),
            gates_all[...],
            (((1,), (1,)), ((), ())),
            preferred_element_type=F32,
        )
    for a in (HERE, NEXT):
        for i in four:
            gather[i]["b", streams[i][3], a].wait_recv()
    routed(0, 12 * HALF)
    to_twin[1].wait_recv()
    to_twin[2].wait_recv()
    shared(PREV)
    shared(NEXT)
    for i in four:
        pass_b(i, FAR)
    ring[2].wait_recv()
    ring[3].wait_recv()
    to_twin.append(copies.start(sx(FAR, 0), sx(FAR, 1), twin))

    groups = ((1, PREV), (0, HERE))
    phases = (
        (pl.ds(0, EARLY), pl.ds(LEFT, EARLY)),
        (pl.ds(EARLY, LEFT - EARLY), pl.ds(LEFT + EARLY, LEFT - EARLY)),
    )

    def yb(b, h, a, n, cols):
        return ys.at[pl.ds(row(b, h, a), n * HALF), cols]

    def spot(g):
        return pl.ds(2 * g * HALF, 2 * HALF)

    reduce = [{} for _ in streams]

    def direct(g, a):
        for i in four:
            h, cols, near, next_, af, ab, bf, bb = streams[i]
            reduce[i]["behind", g] = copies.start(
                yb(near, h, a, 2, cols), behind.at[h, spot(g), cols], bb
            )

    direct(0, HERE)
    for a in (PREV, FAR):
        for i in four:
            gather[i]["b", streams[i][3], a].wait_recv()
    routed(20 * HALF, 12 * HALF)
    direct(1, PREV)
    to_twin[3].wait_recv()
    shared(FAR)
    for i in four:
        for a in four:
            gather[i]["b", FAR, a].wait_recv()
    experts(12 * HALF, 8 * HALF)
    for q in range(2):
        for cols in phases[q]:
            down(12 * HALF, 8 * HALF, cols)
        for g, a in groups:
            for i in four:
                h, _, near, next_, af, ab, bf, bb = streams[i]
                cols = phases[q][i % 2]
                reduce[i]["far", q, g] = copies.start(
                    yb(FAR, h, a, 2, cols), r1.at[h, spot(g), cols], bf
                )

    def sp(dz):
        return shp.at[pl.ds(dz * 2 * TOK, TOK)]

    every = pl.ds(0, D)
    for dz in (FAR, NEXT, PREV, HERE):
        sums[dz].wait_recv()
        add_rows(shp, dz * 2 * TOK, TOK, every, [(sib, dz * TOK)])
        if dz == FAR:
            zs = [
                copies.start(part(sp(FAR), lo), part(u1, lo), zp),
                copies.start(part(sp(FAR), hi), part(u1, hi), zm),
            ]

    for q in range(2):
        for g, a in groups:
            for i in four:
                h, _, near, next_, af, ab, bf, bb = streams[i]
                cols = phases[q][i % 2]
                reduce[i]["far", q, g].wait_recv()
                add_rows(ys, row(next_, h, a), 2 * HALF, cols, [(r1.at[h], 2 * g * HALF)])
                reduce[i]["ahead", q, g] = copies.start(
                    yb(next_, h, a, 2, cols), ahead.at[h, spot(g), cols], bf
                )
    zs[0].wait_recv()
    add_rows(shp, NEXT * 2 * TOK, TOK, lo, [(u1, 0)])
    zs.append(copies.start(sp(NEXT), u2.at[0], zp))
    zs[1].wait_recv()
    add_rows(shp, PREV * 2 * TOK, TOK, hi, [(u1, 0)])
    zs.append(copies.start(sp(PREV), u2.at[1], zm))

    def end_b(q):
        for g, a in groups:
            for i in four:
                h, _, near, next_, af, ab, bf, bb = streams[i]
                cols = phases[q][i % 2]
                if q == 0:
                    reduce[i]["behind", g].wait_recv()
                reduce[i]["ahead", q, g].wait_recv()
                add_rows(
                    ys,
                    row(HERE, h, a),
                    2 * HALF,
                    cols,
                    [(ahead.at[h], 2 * g * HALF), (behind.at[h], 2 * g * HALF)],
                )
                if g == 1:
                    reduce[i]["a far", q] = copies.start(
                        yb(HERE, h, FAR, 1, cols),
                        t1.at[h, :, cols],
                        af if q == 0 else (xf, yf)[h],
                    )
                if q == 1 and next_ in (a, a + 1):
                    reduce[i]["a ahead", q] = copies.start(
                        yb(HERE, h, next_, 1, cols), tahead.at[h, :, cols], af
                    )
                if near in (a, a + 1):
                    reduce[i]["a behind", q] = copies.start(
                        yb(HERE, h, near, 1, cols), tbehind.at[h, :, cols], ab
                    )

    def pass_a(q):
        for i in four:
            h, _, near, next_, af, ab, bf, bb = streams[i]
            cols = phases[q][i % 2]
            reduce[i]["a far", q].wait_recv()
            add_rows(ys, row(HERE, h, next_), HALF, cols, [(t1.at[h], 0)])
            reduce[i]["a ahead", q] = copies.start(
                yb(HERE, h, next_, 1, cols), tahead.at[h, :, cols], af
            )

    home = [[], []]
    spans = (slice(0, 2 * EARLY), slice(2 * EARLY, D))

    def end_a(q):
        for h in range(2):
            first = row(HERE, h, HERE)
            rows = slice(h * 64, h * 64 + 64)
            for i in (2 * h, 2 * h + 1):
                reduce[i]["a behind", q].wait_recv()
                reduce[i]["a ahead", q].wait_recv()
                terms = [(tahead.at[h], 0), (tbehind.at[h], 0)]
                if q == 1:
                    reduce[i]["a far", q].wait_recv()
                    terms.append((t1.at[h], 0))
                cols = phases[q][i % 2]
                add_rows(ys, first, HALF, cols, terms)
                at = pl.ds(spans[q].start + i % 2 * cols.size, cols.size)
                back[rows, at] = jnp.dot(
                    spread, ys[first : first + HALF, cols], preferred_element_type=F32
                ).astype(BF16)
            cols = pl.ds(spans[q].start, spans[q].stop - spans[q].start)
            for p in range(4 * h, 4 * h + 4):
                piece = pl.ds(p * PIECE, PIECE)
                if p:
                    home[q].append(
                        copies.start(back.at[piece, cols], ret.at[piece, cols], ep_from[ORDER[p]])
                    )
                else:
                    ret[piece, cols] = back[piece, cols]

    stores = []

    def finish(q):
        for copy in home[q]:
            copy.wait_recv()
        for i in range(2):
            cols = phases[q][i]
            at = pl.ds(spans[q].start + i * cols.size, cols.size)
            total = lax.dot_general(
                place, ret[:, at], (((0,), (0,)), ((), ())), preferred_element_type=F32
            )
            total += shp[0:TOK, cols].astype(F32)
            total += u2[0, :, cols].astype(F32) + u2[1, :, cols].astype(F32)
            out_ref[:, cols] = total.astype(BF16)
            stores.append(load(out_ref.at[:, cols], out_hbm.at[:, cols]))

    end_b(0)
    pass_a(0)
    end_b(1)
    end_a(0)
    end_a(1)
    for copy in zs[2:]:
        copy.wait_recv()
    finish(0)
    finish(1)

    for copy in copies.made:
        copy.wait_send()
    for copy in stores:
        copy.wait()


def local(
    tokens,
    expert_ids,
    devices,
    slots,
    gates,
    w_gate,
    w_up,
    w_down,
    shared_gate,
    shared_up,
    shared_down,
):
    anywhere = pl.BlockSpec(memory_space=pl.ANY)
    copies = 7 + 60 + 6 + 4 + 4 + 64 + 4 + 4 + 14
    return pl.pallas_call(
        kernel,
        out_shape=jax.ShapeDtypeStruct((TOK, D), BF16),
        in_specs=[anywhere] * 11,
        out_specs=anywhere,
        scratch_shapes=[
            pltpu.VMEM((6, TOK), jnp.int32),
            pltpu.VMEM((3, TOK), jnp.int32),
            pltpu.VMEM((3, TOK), jnp.int32),
            pltpu.VMEM((6, TOK), F32),
            pltpu.VMEM((TOK, D), BF16),
            pltpu.VMEM((3, D, 256), BF16),
            pltpu.VMEM((384, D), BF16),
            pltpu.VMEM((D, 2 * SH), BF16),
            pltpu.VMEM((D, SH), BF16),
            pltpu.VMEM((TOK, MAIN + 128), BF16),
            pltpu.VMEM((TOK, MAIN + 128), BF16),
            pltpu.VMEM((256, 128), BF16),
            pltpu.VMEM((2, HALF, 256), F32),
            pltpu.VMEM((32 * HALF, D), BF16),
            pltpu.VMEM((32 * HALF, D), BF16),
            pltpu.VMEM((12 * HALF, 384), BF16),
            pltpu.VMEM((2, 4 * HALF, D), BF16),
            pltpu.VMEM((2, 4 * HALF, D), BF16),
            pltpu.VMEM((2, 4 * HALF, D), BF16),
            pltpu.VMEM((2, HALF, D), BF16),
            pltpu.VMEM((2, HALF, D), BF16),
            pltpu.VMEM((2, HALF, D), BF16),
            pltpu.VMEM((TOK, D), BF16),
            pltpu.VMEM((TOK, D), BF16),
            pltpu.VMEM((8 * TOK, D), BF16),
            pltpu.VMEM((8 * TOK, D), BF16),
            pltpu.VMEM((2 * TOK, SH), BF16),
            pltpu.VMEM((4 * TOK, D), BF16),
            pltpu.VMEM((TOK, D), BF16),
            pltpu.VMEM((2, TOK, D), BF16),
            pltpu.SemaphoreType.DMA((copies,)),
            pltpu.SemaphoreType.DMA((copies,)),
            pltpu.SemaphoreType.DMA((24,)),
        ],
        compiler_params=pltpu.CompilerParams(
            collective_id=0, has_side_effects=True, vmem_limit_bytes=62 * 1024 * 1024
        ),
        cost_estimate=pl.CostEstimate(
            flops=13_100_000_000, bytes_accessed=12_000_000, transcendentals=900_000
        ),
    )(
        expert_ids.T,
        devices.T,
        slots.T,
        gates.T,
        tokens,
        w_gate,
        w_up,
        w_down,
        shared_gate,
        shared_up,
        shared_down,
    )


def solution(mesh):
    in_specs = (
        P(("seq", "ep"), None),
        P(("seq", "ep"), None),
        P(("seq", "ep"), None),
        P(("seq", "ep"), None),
        P(("seq", "ep"), None),
        P("ep", None, "seq"),
        P("ep", None, "seq"),
        P("ep", "seq", None),
        P(None, "ep"),
        P(None, "ep"),
        P(None, "ep"),
    )
    out_specs = P(("seq", "ep"), None)
    return jax.shard_map(local, mesh=mesh, in_specs=in_specs, out_specs=out_specs, check_vma=False)
```

```python
import functools

import jax
import jax.numpy as jnp
from jax import lax
from jax.experimental import pallas as pl
from jax.experimental.pallas import tpu as pltpu
from jax.sharding import PartitionSpec as P

MESH = pl.DeviceIdType.MESH
F32 = jnp.float32
BF16 = jnp.bfloat16

SIDE = 4
N_EP = 8
TOK = 128
D = 2560
CAP = 12
PIECE = 16
HALF = 4 * CAP
SH = 256
LEFT = 1280
MAIN = 1920
TAIL = D - MAIN
EARLY = 1024
ORDER = (0, 1, 2, 7, 6, 3, 4, 5)

HERE, NEXT, PREV, FAR = 0, 1, 2, 3


class Copies:
    def __init__(self, send, recv):
        self.send, self.recv, self.made = send, recv, []

    def start(self, src, dst, device):
        i = len(self.made)
        copy = pltpu.make_async_remote_copy(
            src_ref=src,
            dst_ref=dst,
            send_sem=self.send.at[i],
            recv_sem=self.recv.at[i],
            device_id=device,
            device_id_type=MESH,
        )
        copy.start()
        self.made.append(copy)
        return copy


def add_rows(dst, start, rows, cols, terms):
    step = 48 if rows % 48 == 0 else 32

    @pl.loop(0, rows // step)
    def _(i):
        at = pl.ds(pl.multiple_of(start + i * step, 16), step)
        total = dst[at, cols].astype(F32)
        for ref, first in terms:
            total += ref[pl.ds(pl.multiple_of(first + i * step, 16), step), cols].astype(F32)
        dst[at, cols] = total.astype(BF16)


def row(b, h, a):
    pair = a // 2
    return (((pair * 4 + (b + pair) % 4) * 2 + h) * 2 + a % 2) * HALF


def kernel(
    ids_hbm,
    dev_hbm,
    slot_hbm,
    gates_hbm,
    tok_hbm,
    wg_hbm,
    wu_hbm,
    wd_hbm,
    sg_hbm,
    su_hbm,
    sd_hbm,
    out_hbm,
    ids_ref,
    dev_ref,
    slot_ref,
    gates_ref,
    out_ref,
    wgu,
    wd,
    sgu,
    sd,
    send,
    land,
    gates_all,
    gate_cols,
    xs,
    ys,
    hid,
    r1,
    ahead,
    behind,
    t1,
    tahead,
    tbehind,
    back,
    ret,
    shx,
    shp,
    shh,
    sib,
    u1,
    u2,
    send_sem,
    recv_sem,
    local_sem,
):
    seq, ep = lax.axis_index("seq"), lax.axis_index("ep")
    y, x = seq // SIDE, lax.rem(seq, SIDE)
    z, core = ep // 2, lax.rem(ep, 2)

    def up(v, by):
        return lax.rem(v + by, SIDE)

    xp, xm = (y * SIDE + up(x, 1), ep), (y * SIDE + up(x, 3), ep)
    yp, ym = (up(y, 1) * SIDE + x, ep), (up(y, 3) * SIDE + x, ep)
    zp, zm = (seq, up(z, 1) * 2 + core), (seq, up(z, 3) * 2 + core)
    twin = (seq, z * 2 + 1 - core)
    ep_to = [(seq, lax.rem(ep + r, N_EP)) for r in range(N_EP)]
    ep_from = [(seq, lax.rem(ep + N_EP - r, N_EP)) for r in range(N_EP)]
    rings = [((xp, xm), (yp, ym)), ((yp, ym), (xp, xm))]
    xf, yf = (y * SIDE + up(x, 2), ep), (up(y, 2) * SIDE + x, ep)

    barrier = pltpu.get_barrier_semaphore()
    partners = [xp, xm, xf, yp, ym, yf] + ep_to[1:]
    for device in partners:
        pl.semaphore_signal(barrier, inc=1, device_id=device, device_id_type=MESH)

    loads = []

    def load(src, dst):
        copy = pltpu.make_async_copy(src, dst, local_sem.at[len(loads)])
        copy.start()
        loads.append(copy)
        return copy

    tok = shx.at[pl.ds(0, TOK)]
    load_small = [
        load(ids_hbm, ids_ref),
        load(dev_hbm, dev_ref),
        load(slot_hbm, slot_ref),
        load(gates_hbm, gates_ref),
    ]
    load_tok = load(tok_hbm, tok)
    load_routed = []
    for k in range(3):
        load_routed.append(load(wg_hbm.at[k], wgu.at[k, :, pl.ds(0, 128)]))
        load_routed.append(load(wu_hbm.at[k], wgu.at[k, :, pl.ds(128, 128)]))
        load_routed.append(load(wd_hbm.at[k], wd.at[pl.ds(k * 128, 128)]))
    load_shared = [
        load(sg_hbm, sgu.at[:, pl.ds(0, SH)]),
        load(su_hbm, sgu.at[:, pl.ds(SH, SH)]),
        load(sd_hbm, sd),
    ]

    rows_i = lax.broadcasted_iota(jnp.int32, (TOK, TOK), 0)
    lanes_i = lax.broadcasted_iota(jnp.int32, (TOK, TOK), 1)
    for copy in load_small:
        copy.wait()
    place = jnp.zeros((TOK, TOK), F32)
    place_tail = [jnp.zeros((TOK, TOK), F32) for _ in range(3)]
    gate_of = [jnp.zeros((TOK, TOK), F32) for _ in range(3)]
    for j in range(3):
        dev = dev_ref[j : j + 1, :]
        slot = slot_ref[j : j + 1, :]
        turn = dev - ep
        turn = jnp.where(turn < 0, turn + N_EP, turn)
        piece = jnp.where(turn < 3, turn, jnp.where(turn < 6, turn + 2, 10 - turn))
        hit = rows_i == jnp.where(slot >= 0, piece * PIECE + slot, -1)
        place = jnp.where(hit, 1.0, place)
        for g in range(3):
            mine = (slot >= 4 * g) & (slot < 4 * g + 4)
            tail_row = jnp.where(mine, piece * PIECE + CAP - 4 * g + slot, -1)
            place_tail[g] = jnp.where(rows_i == tail_row, 1.0, place_tail[g])
        for k in range(3):
            summed = jnp.zeros((1, TOK), F32)
            for r in range(6):
                summed += jnp.where(
                    ids_ref[r : r + 1, :] == dev * 3 + k, gates_ref[r : r + 1, :], 0.0
                )
            gate_of[k] = jnp.where(hit, summed, gate_of[k])
    place = place.astype(BF16)
    place_tail = [p.astype(BF16) for p in place_tail]
    columns = jnp.zeros((TOK, TOK), F32)
    for k in range(3):
        column = jnp.sum(gate_of[k], axis=1, keepdims=True)
        columns = jnp.where(lanes_i == k, column, columns)
    send[:, MAIN:] = columns.astype(BF16)

    load_tok.wait()
    for g in range(3):
        cols = slice(g * TAIL, (g + 1) * TAIL)
        send[:, cols] = (
            jnp.dot(place, shx[0:TOK, cols], preferred_element_type=F32)
            + jnp.dot(place_tail[g], shx[0:TOK, MAIN:], preferred_element_type=F32)
        ).astype(BF16)

    pl.semaphore_wait(barrier, len(partners))
    copies = Copies(send_sem, recv_sem)

    def sx(dz, c):
        return shx.at[pl.ds((dz * 2 + c) * TOK, TOK)]

    arrive = [None]

    def exchange(first, end):
        for p in range(first, end):
            piece = pl.ds(p * PIECE, PIECE)
            arrive.append(copies.start(send.at[piece], land.at[piece], ep_to[ORDER[p]]))

    exchange(1, 4)
    land[0:PIECE, :] = send[0:PIECE, :]
    to_twin = [copies.start(sx(HERE, 0), sx(HERE, 1), twin)]

    def dense(flip, g=None):
        shape = (4 * PIECE, HALF) if flip else (HALF, 4 * PIECE)
        one = lax.broadcasted_iota(jnp.int32, shape, 1 if flip else 0)
        two = lax.broadcasted_iota(jnp.int32, shape, 0 if flip else 1)
        hit = jnp.zeros(shape, F32)
        for i in range(4):
            first, count, shift = CAP * i, CAP, (PIECE - CAP) * i
            if g is not None:
                first, count, shift = first + 4 * g, 4, shift + CAP - 4 * g
            inside = (one >= first) & (one < first + count) & (two == one + shift)
            hit = jnp.where(inside, 1.0, hit)
        return hit.astype(BF16)

    squeeze, squeeze_tail = dense(False), [dense(False, g) for g in range(3)]
    spread = dense(True)

    lo, hi = pl.ds(0, LEFT), pl.ds(LEFT, D - LEFT)

    def xb(b, h, a, cols):
        return xs.at[pl.ds(row(b, h, a), HALF), cols]

    streams = []
    for h in range(2):
        (ap, am), (bp, bm) = rings[h]
        streams.append((h, lo, PREV, NEXT, ap, am, bp, bm))
        streams.append((h, hi, NEXT, PREV, am, ap, bm, bp))

    gather = [{} for _ in streams]
    for h in range(2):
        for p in range(4 * h, 4 * h + 4):
            if p:
                arrive[p].wait_recv()
        if h == 0:
            exchange(4, 8)
        first = row(HERE, h, HERE)
        rows = slice(h * 64, h * 64 + 64)
        for g in range(3):
            cols = slice(g * TAIL, (g + 1) * TAIL)
            xs[first : first + HALF, cols] = jnp.dot(
                squeeze, land[rows, cols], preferred_element_type=F32
            ).astype(BF16)
        tail = jnp.zeros((HALF, TAIL), F32)
        for g in range(3):
            cols = slice(g * TAIL, (g + 1) * TAIL)
            tail += jnp.dot(squeeze_tail[g], land[rows, cols], preferred_element_type=F32)
        xs[first : first + HALF, MAIN:D] = tail.astype(BF16)
        for i in (2 * h, 2 * h + 1):
            _, cols, near, next_, af, ab, bf, bb = streams[i]
            own, got = xb(HERE, h, HERE, cols), gather[i]
            got["a", near] = copies.start(own, xb(HERE, h, near, cols), af)
            got["b", near, HERE] = copies.start(own, xb(near, h, HERE, cols), bf)
        for i in (2 * h, 2 * h + 1):
            _, cols, near, next_, af, ab, bf, bb = streams[i]
            own, got = xb(HERE, h, HERE, cols), gather[i]
            got["a", next_] = copies.start(own, xb(HERE, h, next_, cols), ab)
            got["b", next_, HERE] = copies.start(own, xb(next_, h, HERE, cols), bb)

    lands = lax.broadcasted_iota(jnp.int32, (TOK, TOK), 0)
    slots_i = lax.broadcasted_iota(jnp.int32, (TOK, TOK), 1)
    which = jnp.zeros((TOK, TOK), F32)
    for p in range(N_EP):
        inside = (slots_i >= CAP * p) & (slots_i < CAP * (p + 1))
        which = jnp.where(inside & (lands == slots_i + (PIECE - CAP) * p), 1.0, which)
    turned = lax.dot_general(
        land[:, MAIN:],
        which.astype(BF16),
        (((0,), (0,)), ((), ())),
        preferred_element_type=F32,
    )
    gates_all[0:16, :] = turned[0:16, :].astype(BF16)

    def tiles(ry, rx, n):
        return gates_all.at[pl.ds((ry * 4 + rx) * 16, n * 16)]

    gate_copies = [
        copies.start(tiles(HERE, HERE, 1), tiles(HERE, PREV, 1), xp),
        copies.start(tiles(HERE, HERE, 1), tiles(HERE, NEXT, 1), xm),
        copies.start(tiles(HERE, HERE, 1), tiles(HERE, FAR, 1), xf),
    ]

    ring = [
        copies.start(sx(HERE, 0), sx(PREV, 0), zp),
        copies.start(sx(HERE, 0), sx(NEXT, 0), zm),
    ]

    def part(ref, cols):
        return ref.at[:, cols]

    def along_b(i, a):
        h, cols, near, next_, af, ab, bf, bb = streams[i]
        gather[i]["b", near, a] = copies.start(xb(HERE, h, a, cols), xb(near, h, a, cols), bf)
        gather[i]["b", next_, a] = copies.start(xb(HERE, h, a, cols), xb(next_, h, a, cols), bb)

    def pass_b(i, a):
        h, cols, near, next_, af, ab, bf, bb = streams[i]
        gather[i]["b", near, a].wait_recv()
        gather[i]["b", FAR, a] = copies.start(xb(near, h, a, cols), xb(FAR, h, a, cols), bf)

    sums = {}

    def shared(dz):
        at = pl.ds(dz * 2 * TOK, 2 * TOK)
        both = jnp.dot(shx[at, :], sgu[...], preferred_element_type=F32)
        shh[...] = (jax.nn.silu(both[:, :SH]) * both[:, SH:]).astype(BF16)

        @pl.loop(0, D // 512)
        def _(n):
            cols = pl.ds(pl.multiple_of(n * 512, 512), 512)
            shp[at, cols] = lax.dot_general(
                shh[...], sd[cols, :], (((1,), (1,)), ((), ())), preferred_element_type=F32
            ).astype(BF16)

        sums[dz] = copies.start(
            shp.at[pl.ds((dz * 2 + 1) * TOK, TOK)], sib.at[pl.ds(dz * TOK, TOK)], twin
        )

    for copy in load_shared:
        copy.wait()
    to_twin[0].wait_recv()
    shared(HERE)

    four = range(4)
    for i in four:
        h, cols, near, next_, af, ab, bf, bb = streams[i]
        gather[i]["a", near].wait_recv()
        gather[i]["a", FAR] = copies.start(xb(HERE, h, near, cols), xb(HERE, h, FAR, cols), af)
        along_b(i, near)
    for i in four:
        pass_b(i, HERE)
    for i in four:
        gather[i]["a", streams[i][3]].wait_recv()
        along_b(i, streams[i][3])
    for copy in gate_copies[:3]:
        copy.wait_recv()
    gate_copies += [
        copies.start(tiles(HERE, HERE, 4), tiles(PREV, HERE, 4), yp),
        copies.start(tiles(HERE, HERE, 4), tiles(NEXT, HERE, 4), ym),
        copies.start(tiles(HERE, HERE, 4), tiles(FAR, HERE, 4), yf),
    ]
    for i in four:
        gather[i]["a", FAR].wait_recv()
        along_b(i, FAR)

    def experts(start, rows):
        spots = {row(b, h, a): (h, a, b) for b in four for h in range(2) for a in four}
        columns = []
        for first in range(start, start + rows, HALF):
            h, a, b = spots[first]
            columns.append((h, (b * 4 + a if h == 0 else a * 4 + b) * 16))
        at = pl.ds(start, rows)
        for k in range(3):
            both = jnp.dot(xs[at, :], wgu[k], preferred_element_type=F32)
            gate = jnp.concatenate([gate_cols[h, :, c + k : c + k + 1] for h, c in columns], 0)
            value = jax.nn.silu(both[:, :128]) * both[:, 128:] * gate
            hid[0:rows, k * 128 : (k + 1) * 128] = value.astype(BF16)

    def down(start, rows, cols):
        ys[pl.ds(start, rows), cols] = jnp.dot(
            hid[0:rows, :], wd[:, cols], preferred_element_type=F32
        ).astype(BF16)

    def routed(start, rows):
        experts(start, rows)

        @pl.loop(0, D // 512)
        def _(n):
            down(start, rows, pl.ds(pl.multiple_of(n * 512, 512), 512))

    groups = ((1, PREV), (0, HERE))
    phases = (
        (pl.ds(0, EARLY), pl.ds(LEFT, EARLY)),
        (pl.ds(EARLY, LEFT - EARLY), pl.ds(LEFT + EARLY, LEFT - EARLY)),
    )

    def yb(b, h, a, n, cols):
        return ys.at[pl.ds(row(b, h, a), n * HALF), cols]

    def spot(g):
        return pl.ds(2 * g * HALF, 2 * HALF)

    reduce = [{} for _ in streams]

    def direct(g, a):
        for i in four:
            h, cols, near, next_, af, ab, bf, bb = streams[i]
            reduce[i]["behind", g] = copies.start(
                yb(near, h, a, 2, cols), behind.at[h, spot(g), cols], bb
            )

    for i in four:
        pass_b(i, streams[i][2])
    for i in four:
        pass_b(i, streams[i][3])
    ring[0].wait_recv()
    ring.append(copies.start(part(sx(PREV, 0), lo), part(sx(FAR, 0), lo), zp))
    to_twin.append(copies.start(sx(PREV, 0), sx(PREV, 1), twin))
    ring[1].wait_recv()
    ring.append(copies.start(part(sx(NEXT, 0), hi), part(sx(FAR, 0), hi), zm))
    to_twin.append(copies.start(sx(NEXT, 0), sx(NEXT, 1), twin))
    for copy in load_routed:
        copy.wait()
    for copy in gate_copies[3:]:
        copy.wait_recv()
    for h in range(2):
        spots = lax.broadcasted_iota(jnp.int32, (HALF, TOK), 1) == (
            lax.broadcasted_iota(jnp.int32, (HALF, TOK), 0) + h * HALF
        )
        gate_cols[h] = lax.dot_general(
            jnp.where(spots, 1.0, 0.0).astype(BF16),
            gates_all[...],
            (((1,), (1,)), ((), ())),
            preferred_element_type=F32,
        )
    for a in (HERE, NEXT):
        for i in four:
            gather[i]["b", streams[i][3], a].wait_recv()
    routed(0, 12 * HALF)
    direct(0, HERE)
    to_twin[1].wait_recv()
    to_twin[2].wait_recv()
    shared(PREV)
    shared(NEXT)
    for i in four:
        pass_b(i, FAR)
    ring[2].wait_recv()
    ring[3].wait_recv()
    to_twin.append(copies.start(sx(FAR, 0), sx(FAR, 1), twin))

    for a in (PREV, FAR):
        for i in four:
            gather[i]["b", streams[i][3], a].wait_recv()
    routed(20 * HALF, 12 * HALF)
    direct(1, PREV)
    to_twin[3].wait_recv()
    shared(FAR)
    for i in four:
        for a in four:
            gather[i]["b", FAR, a].wait_recv()
    experts(12 * HALF, 8 * HALF)
    for q in range(2):
        for cols in phases[q]:
            down(12 * HALF, 8 * HALF, cols)
        for g, a in groups:
            for i in four:
                h, _, near, next_, af, ab, bf, bb = streams[i]
                cols = phases[q][i % 2]
                reduce[i]["far", q, g] = copies.start(
                    yb(FAR, h, a, 2, cols), r1.at[h, spot(g), cols], bf
                )

    def sp(dz):
        return shp.at[pl.ds(dz * 2 * TOK, TOK)]

    every = pl.ds(0, D)
    for dz in (FAR, NEXT, PREV, HERE):
        sums[dz].wait_recv()
        add_rows(shp, dz * 2 * TOK, TOK, every, [(sib, dz * TOK)])
        if dz == FAR:
            zs = [
                copies.start(part(sp(FAR), lo), part(u1, lo), zp),
                copies.start(part(sp(FAR), hi), part(u1, hi), zm),
            ]

    for q in range(2):
        for g, a in groups:
            for i in four:
                h, _, near, next_, af, ab, bf, bb = streams[i]
                cols = phases[q][i % 2]
                reduce[i]["far", q, g].wait_recv()
                add_rows(ys, row(next_, h, a), 2 * HALF, cols, [(r1.at[h], 2 * g * HALF)])
                reduce[i]["ahead", q, g] = copies.start(
                    yb(next_, h, a, 2, cols), ahead.at[h, spot(g), cols], bf
                )
    zs[0].wait_recv()
    add_rows(shp, NEXT * 2 * TOK, TOK, lo, [(u1, 0)])
    zs.append(copies.start(sp(NEXT), u2.at[0], zp))
    zs[1].wait_recv()
    add_rows(shp, PREV * 2 * TOK, TOK, hi, [(u1, 0)])
    zs.append(copies.start(sp(PREV), u2.at[1], zm))

    def end_b(q):
        for g, a in groups:
            for i in four:
                h, _, near, next_, af, ab, bf, bb = streams[i]
                cols = phases[q][i % 2]
                if q == 0:
                    reduce[i]["behind", g].wait_recv()
                reduce[i]["ahead", q, g].wait_recv()
                add_rows(
                    ys,
                    row(HERE, h, a),
                    2 * HALF,
                    cols,
                    [(ahead.at[h], 2 * g * HALF), (behind.at[h], 2 * g * HALF)],
                )
                if g == 1:
                    reduce[i]["a far", q] = copies.start(
                        yb(HERE, h, FAR, 1, cols),
                        t1.at[h, :, cols],
                        af if q == 0 else (xf, yf)[h],
                    )
                if q == 1 and next_ in (a, a + 1):
                    reduce[i]["a ahead", q] = copies.start(
                        yb(HERE, h, next_, 1, cols), tahead.at[h, :, cols], af
                    )
                if near in (a, a + 1):
                    reduce[i]["a behind", q] = copies.start(
                        yb(HERE, h, near, 1, cols), tbehind.at[h, :, cols], ab
                    )

    def pass_a(q):
        for i in four:
            h, _, near, next_, af, ab, bf, bb = streams[i]
            cols = phases[q][i % 2]
            reduce[i]["a far", q].wait_recv()
            add_rows(ys, row(HERE, h, next_), HALF, cols, [(t1.at[h], 0)])
            reduce[i]["a ahead", q] = copies.start(
                yb(HERE, h, next_, 1, cols), tahead.at[h, :, cols], af
            )

    home = [[], []]
    spans = (slice(0, 2 * EARLY), slice(2 * EARLY, D))

    def end_a(q):
        for h in range(2):
            first = row(HERE, h, HERE)
            rows = slice(h * 64, h * 64 + 64)
            for i in (2 * h, 2 * h + 1):
                reduce[i]["a behind", q].wait_recv()
                reduce[i]["a ahead", q].wait_recv()
                terms = [(tahead.at[h], 0), (tbehind.at[h], 0)]
                if q == 1:
                    reduce[i]["a far", q].wait_recv()
                    terms.append((t1.at[h], 0))
                cols = phases[q][i % 2]
                add_rows(ys, first, HALF, cols, terms)
                at = pl.ds(spans[q].start + i % 2 * cols.size, cols.size)
                back[rows, at] = jnp.dot(
                    spread, ys[first : first + HALF, cols], preferred_element_type=F32
                ).astype(BF16)
            cols = pl.ds(spans[q].start, spans[q].stop - spans[q].start)
            for p in range(4 * h, 4 * h + 4):
                piece = pl.ds(p * PIECE, PIECE)
                if p:
                    home[q].append(
                        copies.start(back.at[piece, cols], ret.at[piece, cols], ep_from[ORDER[p]])
                    )
                else:
                    ret[piece, cols] = back[piece, cols]

    stores = []

    def finish(q):
        for copy in home[q]:
            copy.wait_recv()
        for i in range(2):
            cols = phases[q][i]
            at = pl.ds(spans[q].start + i * cols.size, cols.size)
            total = lax.dot_general(
                place, ret[:, at], (((0,), (0,)), ((), ())), preferred_element_type=F32
            )
            total += shp[0:TOK, cols].astype(F32)
            total += u2[0, :, cols].astype(F32) + u2[1, :, cols].astype(F32)
            out_ref[:, cols] = total.astype(BF16)
            stores.append(load(out_ref.at[:, cols], out_hbm.at[:, cols]))

    end_b(0)
    pass_a(0)
    end_b(1)
    end_a(0)
    end_a(1)
    for copy in zs[2:]:
        copy.wait_recv()
    finish(0)
    finish(1)

    for copy in copies.made:
        copy.wait_send()
    for copy in stores:
        copy.wait()


def local(
    tokens,
    expert_ids,
    devices,
    slots,
    gates,
    w_gate,
    w_up,
    w_down,
    shared_gate,
    shared_up,
    shared_down,
):
    anywhere = pl.BlockSpec(memory_space=pl.ANY)
    copies = 7 + 60 + 6 + 4 + 4 + 64 + 4 + 4 + 14
    return pl.pallas_call(
        kernel,
        out_shape=jax.ShapeDtypeStruct((TOK, D), BF16),
        in_specs=[anywhere] * 11,
        out_specs=anywhere,
        scratch_shapes=[
            pltpu.VMEM((6, TOK), jnp.int32),
            pltpu.VMEM((3, TOK), jnp.int32),
            pltpu.VMEM((3, TOK), jnp.int32),
            pltpu.VMEM((6, TOK), F32),
            pltpu.VMEM((TOK, D), BF16),
            pltpu.VMEM((3, D, 256), BF16),
            pltpu.VMEM((384, D), BF16),
            pltpu.VMEM((D, 2 * SH), BF16),
            pltpu.VMEM((D, SH), BF16),
            pltpu.VMEM((TOK, MAIN + 128), BF16),
            pltpu.VMEM((TOK, MAIN + 128), BF16),
            pltpu.VMEM((256, 128), BF16),
            pltpu.VMEM((2, HALF, 256), F32),
            pltpu.VMEM((32 * HALF, D), BF16),
            pltpu.VMEM((32 * HALF, D), BF16),
            pltpu.VMEM((12 * HALF, 384), BF16),
            pltpu.VMEM((2, 4 * HALF, D), BF16),
            pltpu.VMEM((2, 4 * HALF, D), BF16),
            pltpu.VMEM((2, 4 * HALF, D), BF16),
            pltpu.VMEM((2, HALF, D), BF16),
            pltpu.VMEM((2, HALF, D), BF16),
            pltpu.VMEM((2, HALF, D), BF16),
            pltpu.VMEM((TOK, D), BF16),
            pltpu.VMEM((TOK, D), BF16),
            pltpu.VMEM((8 * TOK, D), BF16),
            pltpu.VMEM((8 * TOK, D), BF16),
            pltpu.VMEM((2 * TOK, SH), BF16),
            pltpu.VMEM((4 * TOK, D), BF16),
            pltpu.VMEM((TOK, D), BF16),
            pltpu.VMEM((2, TOK, D), BF16),
            pltpu.SemaphoreType.DMA((copies,)),
            pltpu.SemaphoreType.DMA((copies,)),
            pltpu.SemaphoreType.DMA((24,)),
        ],
        compiler_params=pltpu.CompilerParams(
            collective_id=0, has_side_effects=True, vmem_limit_bytes=62 * 1024 * 1024
        ),
        cost_estimate=pl.CostEstimate(
            flops=13_100_000_000, bytes_accessed=12_000_000, transcendentals=900_000
        ),
    )(
        expert_ids.T,
        devices.T,
        slots.T,
        gates.T,
        tokens,
        w_gate,
        w_up,
        w_down,
        shared_gate,
        shared_up,
        shared_down,
    )


def solution(mesh):
    in_specs = (
        P(("seq", "ep"), None),
        P(("seq", "ep"), None),
        P(("seq", "ep"), None),
        P(("seq", "ep"), None),
        P(("seq", "ep"), None),
        P("ep", None, "seq"),
        P("ep", None, "seq"),
        P("ep", "seq", None),
        P(None, "ep"),
        P(None, "ep"),
        P(None, "ep"),
    )
    out_specs = P(("seq", "ep"), None)
    return jax.shard_map(local, mesh=mesh, in_specs=in_specs, out_specs=out_specs, check_vma=False)
```
